32 devices in a mesh: dp: 4 (over y, x), seq: 8 (over z, core).
Axes of the slice: x: 2, y: 2, z: 4, core: 2. Of those that a mesh axis runs over, the one named last changes fastest.
Arguments:
- queries: bfloat16 [4096, 32, 128], P(('dp', 'seq')), parts along dimension 0, may hold values from -6 to 6
- keys: bfloat16 [4096, 4, 128], P(('dp', 'seq')), parts along dimension 0, may hold values from -6 to 6
- values: bfloat16 [4096, 4, 128], P(('dp', 'seq')), parts along dimension 0, may hold values from -6 to 6
- attn_out: bfloat16 [4096, 32, 128], P(('dp', 'seq')), parts along dimension 0, may hold values from -6 to 6
- out_grad: bfloat16 [4096, 32, 128], P(('dp', 'seq')), parts along dimension 0, may hold values from -1.5 to 1.5
- log_sums: float32 [32, 4096], P(None, ('dp', 'seq')), parts along dimension 1, may hold values from 2 to 4
- doc_ids: int32 [4096], P('dp'), parts along dimension 0, may hold values from 0 to 3, never falling along the last dimension, each value on 1 to 512 neighbouring positions
Outputs:
- query_grad: bfloat16 [4096, 32, 128], P(('dp', 'seq')), parts along dimension 0
- key_grad: bfloat16 [4096, 4, 128], P(('dp', 'seq')), parts along dimension 0
- value_grad: bfloat16 [4096, 4, 128], P(('dp', 'seq')), parts along dimension 0
The draws below stay inside these ranges and needn't reach their ends.
There are 4 independent parts, one for each index of `dp`. The reference program is written for one: setup_inputs(seed, part) draws one part's arguments, and reference() takes and returns one part's arrays. A program takes and returns all parts, laid end to end along the dimension named above; each array names one. Nothing has to cross between parts.
Inputs may be any that keep to these rules, and one draw needn't show every extreme that they name: `doc_ids`: document numbers never fall along the sequence; each document holds 1 to 512 positions, and one holds exactly 512.
All inputs are finite; a program needn't handle non-finite values.
Results may differ from the reference program's by a relative error of at most 0.009.
Values may be sent and summed in bfloat16 or wider, within the bound.
No kernel may reach another device: no remote copies, remote signals or barrier semaphores. Data moves between devices by JAX's collectives and lax.ppermute only.
A program may use at most 64 MiB of HBM per device.

```python
import math
import jax
import jax.numpy as jnp
import numpy as np
from jax import lax

HEADS = 32
KV_HEADS = 4
HD = 128
TOK_DEV = 128
GROUP = 8
REACH = 4
DOC_MOST = 512
SEQ = 1024
DOCS = 4


def shard_levels(own_key, shape, split, least, top_value):
    gain = 1.0
    for dim, parts in split:
        steps = jax.random.uniform(jax.random.fold_in(jax.random.fold_in(own_key, 6), dim), (parts,), jnp.float32, least / len(split), top_value / len(split))
        gain = gain * jnp.repeat(jnp.exp(steps), shape[dim] // parts).reshape((-1,) + (1,) * (len(shape) - 1 - dim))
    return gain


def split_up(count, total, limit, slope):
    weights = [(1 << 20) // math.isqrt(grade ** slope) + 1 for grade in range(2, count + 1)]
    rest, counts = total - limit - (count - 1), [1] * (count - 1)
    while rest > 0:
        free = [i for i in range(count - 1) if counts[i] < limit]
        whole, budget = sum([weights[i] for i in free]), rest
        for i in free:
            more = min(limit - counts[i], max(1, budget * weights[i] // whole), rest)
            counts[i] = counts[i] + more
            rest = rest - more
    return np.array([limit] + counts)


def uneven(own_key, amount, total, limit, slope):
    if amount == 2:
        one = jax.random.randint(own_key, (), max(1, total - limit), min(limit, total - 1) + 1)
        return jnp.stack([one, total - one])
    sizes = jnp.asarray(split_up(amount, total, limit, slope), jnp.int32)
    twos = (amount - 1) // 2
    source_of, sink = sizes[1:1 + 2 * twos:2], sizes[2:2 + 2 * twos:2]
    room = jnp.minimum(source_of - 1, limit - sink)
    moved = jax.random.randint(jax.random.fold_in(own_key, 1), (twos,), 0, 1 << 20) % (room + 1)
    sizes = sizes.at[1:1 + 2 * twos:2].set(source_of - moved).at[2:2 + 2 * twos:2].set(sink + moved)
    return sizes[jax.random.permutation(jax.random.fold_in(own_key, 2), amount)]


def gaussian(stream_key, extent, scale, bound, pieces=(), kind=jnp.bfloat16):
    gain = shard_levels(stream_key, extent, pieces, -0.22, 0.18) if pieces else 1.0
    drawn = jax.random.normal(stream_key, extent, jnp.float32) * scale * gain
    return jnp.minimum(jnp.maximum(drawn, -bound), bound).astype(kind)


def setup_inputs(seed: int = 0, part: int = 0) -> dict:
    key_of = jax.random.split(jax.random.key(seed), 8)
    part_splits = jax.random.split(jax.random.fold_in(key_of[7], part), 8)
    queries = gaussian(part_splits[0], (SEQ, HEADS, HD), 1.0, 6.0, ((0, 8),))
    keys = gaussian(part_splits[1], (SEQ, KV_HEADS, HD), 1.0, 6.0, ((0, 8),))
    values = gaussian(part_splits[2], (SEQ, KV_HEADS, HD), 1.0, 6.0, ((0, 8),))
    attn_out = gaussian(part_splits[3], (SEQ, HEADS, HD), 1.0, 6.0, ((0, 8),))
    out_grad = gaussian(part_splits[4], (SEQ, HEADS, HD), 0.25, 1.5, ((0, 8),))
    log_sums = jnp.clip(2.0 + 2.0 * jax.random.uniform(part_splits[5], (HEADS, SEQ), jnp.float32) ** shard_levels(part_splits[5], (HEADS, SEQ), ((1, 8),), -0.2, 0.2), 2.0, 4.0)
    doc_ids = jnp.searchsorted(jnp.cumsum(uneven(part_splits[6], DOCS, SEQ, DOC_MOST, 1)), jnp.arange(SEQ), side="right").astype(jnp.int32)
    return dict(queries=queries, keys=keys, values=values, attn_out=attn_out, out_grad=out_grad, log_sums=log_sums, doc_ids=doc_ids)


def reference(queries, keys, values, attn_out, out_grad, log_sums, doc_ids):
    width = TOK_DEV
    span = (REACH + 1) * width
    margin = REACH * width
    scale = HD ** -0.5
    hi = lax.Precision.HIGHEST
    delta = jnp.sum(out_grad.astype(jnp.float32) * attn_out.astype(jnp.float32), axis=-1)
    key_pad = jnp.concatenate([jnp.zeros((margin, KV_HEADS, HD), keys.dtype), keys], 0)
    val_pad = jnp.concatenate([jnp.zeros((margin, KV_HEADS, HD), values.dtype), values], 0)
    doc_pad = jnp.concatenate([jnp.full((margin,), -1, jnp.int32), doc_ids.astype(jnp.int32)], 0)
    offsets = jnp.arange(width, dtype=jnp.int32)
    key_offsets = jnp.arange(span, dtype=jnp.int32)

    def block(carry, shard):
        key_acc, val_acc = carry
        start = (shard * width).astype(jnp.int32)
        query_blk = lax.dynamic_slice_in_dim(queries, start, width, 0).astype(jnp.float32).reshape(width, KV_HEADS, GROUP, HD)
        grad_blk = lax.dynamic_slice_in_dim(out_grad, start, width, 0).astype(jnp.float32).reshape(width, KV_HEADS, GROUP, HD)
        lse_blk = lax.dynamic_slice_in_dim(log_sums, start, width, 1).reshape(KV_HEADS, GROUP, width)
        delta_blk = lax.dynamic_slice_in_dim(delta, start, width, 0).T.reshape(KV_HEADS, GROUP, width)
        key_win = lax.dynamic_slice_in_dim(key_pad, start, span, 0).astype(jnp.float32)
        val_win = lax.dynamic_slice_in_dim(val_pad, start, span, 0).astype(jnp.float32)
        query_pos = start + offsets
        key_pos = start - margin + key_offsets
        query_doc = lax.dynamic_slice_in_dim(doc_ids.astype(jnp.int32), start, width, 0)
        key_doc = lax.dynamic_slice_in_dim(doc_pad, start, span, 0)
        live = (key_pos[None, :] <= query_pos[:, None]) & (key_doc[None, :] == query_doc[:, None]) & (key_pos[None, :] >= 0)
        scores = jnp.einsum("tkgd,skd->kgts", query_blk, key_win, precision=hi) * scale
        probs = jnp.where(live, jnp.exp(scores - lse_blk[..., None]), 0.0)
        dprobs = jnp.einsum("tkgd,skd->kgts", grad_blk, val_win, precision=hi)
        dscores = probs * (dprobs - delta_blk[..., None])
        probs_low = lax.optimization_barrier(probs.astype(jnp.bfloat16)).astype(jnp.float32)
        dscores_low = lax.optimization_barrier(dscores.astype(jnp.bfloat16)).astype(jnp.float32)
        query_part = jnp.einsum("kgts,skd->tkgd", dscores_low, key_win, precision=hi) * scale
        key_part = jnp.einsum("kgts,tkgd->skd", dscores_low, query_blk, precision=hi) * scale
        val_part = jnp.einsum("kgts,tkgd->skd", probs_low, grad_blk, precision=hi)
        key_part = lax.optimization_barrier(key_part.astype(jnp.bfloat16)).astype(jnp.float32)
        val_part = lax.optimization_barrier(val_part.astype(jnp.bfloat16)).astype(jnp.float32)
        key_acc = lax.dynamic_update_slice_in_dim(key_acc, lax.dynamic_slice_in_dim(key_acc, start, span, 0) + key_part, start, 0)
        val_acc = lax.dynamic_update_slice_in_dim(val_acc, lax.dynamic_slice_in_dim(val_acc, start, span, 0) + val_part, start, 0)
        return (key_acc, val_acc), query_part.reshape(width, HEADS, HD).astype(jnp.bfloat16)

    start_acc = jnp.zeros((margin + SEQ, KV_HEADS, HD), jnp.float32)
    (key_acc, val_acc), query_grad = lax.scan(block, (start_acc, start_acc), jnp.arange(SEQ // TOK_DEV, dtype=jnp.int32))
    query_grad = query_grad.reshape(SEQ, HEADS, HD)
    return query_grad, key_acc[margin:].astype(jnp.bfloat16), val_acc[margin:].astype(jnp.bfloat16)
```

```python
import functools

import jax
import jax.numpy as jnp
from jax import lax
from jax.experimental import pallas as pl
from jax.experimental.pallas import tpu as pltpu
from jax.sharding import PartitionSpec as P

LOG2E = 1.4426950408889634
VMEM = pl.BlockSpec(memory_space=pltpu.VMEM)
SMEM = pl.BlockSpec(memory_space=pltpu.SMEM)


def params(mib):
    return pltpu.CompilerParams(vmem_limit_bytes=mib * 1024 * 1024)


def split3(value):
    high = value.astype(jnp.bfloat16).astype(jnp.float32)
    rest = value - high
    middle = rest.astype(jnp.bfloat16).astype(jnp.float32)
    return high, middle, rest - middle


def stats_kernel(heads, grad_ref, out_ref, log_ref, aux_ref):
    rows = grad_ref.shape[0]
    delta = jnp.sum(
        grad_ref[...].astype(jnp.float32) * out_ref[...].astype(jnp.float32), axis=-1, keepdims=True
    )
    d_high, d_mid, d_low = split3(delta)
    l_high, l_mid, l_low = split3(log_ref[...])
    lane_row = lax.broadcasted_iota(jnp.int32, (rows, 128), 1)
    logs = jnp.where(
        lane_row < heads, l_high, jnp.where(lane_row < 2 * heads, l_mid, l_low)
    )
    lane = lax.broadcasted_iota(jnp.int32, (1, heads, 128), 2)
    head = lax.broadcasted_iota(jnp.int32, (1, heads, 128), 1)
    own = (lane == head) | (lane == head + heads) | (lane == head + 2 * heads)
    aux = jnp.where(own, logs[:, None, :], 0.0)
    aux = jnp.where(lane == 3 * heads, d_high, aux)
    aux = jnp.where(lane == 3 * heads + 1, d_mid, aux)
    aux = jnp.where(lane == 3 * heads + 2, d_low, aux)
    aux_ref[...] = aux.astype(jnp.bfloat16)


def stats(out_grad, attn_out, logs4):
    rows, heads, size = out_grad.shape
    steps = 4
    big = pl.BlockSpec((rows // steps, heads, size), lambda i: (i, 0, 0))
    return pl.pallas_call(
        functools.partial(stats_kernel, heads),
        grid=(steps,),
        in_specs=[big, big, pl.BlockSpec((rows // steps, 128), lambda i: (i, 0))],
        out_specs=big,
        out_shape=jax.ShapeDtypeStruct((rows, heads, 128), jnp.bfloat16),
        compiler_params=params(16),
        name="stats",
    )(out_grad, attn_out, logs4)


def chunk_kernel(
    scale, info_ref, end_ref, q0, g0, a0, q1, g1, a1, k_ref, v_ref, ds_ref, dk_ref, dv_ref, dk_acc, dv_acc
):
    rows, heads, size = q0.shape
    kv_count = k_ref.shape[1]
    group = heads // kv_count
    count = rows * group
    width = k_ref.shape[0]
    dk_acc[...] = jnp.zeros_like(dk_acc)
    dv_acc[...] = jnp.zeros_like(dv_acc)
    key_start = info_ref[0]
    last_end = info_ref[3]
    lane = lax.broadcasted_iota(jnp.int32, (width, 128), 1)
    log_cols = jnp.where(lane < 3 * heads, -1.0, 0.0).astype(jnp.bfloat16)
    delta_cols = jnp.where((lane >= 3 * heads) & (lane < 3 * heads + 3), -1.0, 0.0).astype(jnp.bfloat16)
    for side, (q_ref, g_ref, a_ref) in enumerate(((q0, g0, a0), (q1, g1, a1))):
        start = info_ref[1 + side]
        live = (key_start < start + rows) & (last_end >= start)

        @pl.when(live)
        def _():
            pos = start + lax.broadcasted_iota(jnp.int32, (rows, group, width), 0).reshape(count, width)
            key_pos = key_start + lax.broadcasted_iota(jnp.int32, (1, width), 1)
            mask = (pos >= key_pos) & (pos <= end_ref[...])
            for kv in range(kv_count):
                span = slice(kv * group, (kv + 1) * group)
                query = q_ref[:, span, :].reshape(count, size)
                grad = g_ref[:, span, :].reshape(count, size)
                aux = a_ref[:, span, :].reshape(count, 128)
                key = jnp.concatenate([k_ref[:, kv, :], log_cols], axis=1)
                val = jnp.concatenate([v_ref[:, kv, :], delta_cols], axis=1)
                nt = (((1,), (1,)), ((), ()))
                tn = (((0,), (0,)), ((), ()))
                logits = lax.dot_general(
                    jnp.concatenate([query, aux], axis=1), key, nt, preferred_element_type=jnp.float32
                )
                probs = jnp.where(mask, jnp.exp2(logits * (scale * LOG2E)), 0.0)
                diff = lax.dot_general(
                    jnp.concatenate([grad, aux], axis=1), val, nt, preferred_element_type=jnp.float32
                )
                ds = (probs * diff).astype(jnp.bfloat16)
                ds_ref[side, kv] = ds
                dv_acc[kv] += lax.dot_general(
                    probs.astype(jnp.bfloat16), grad, tn, preferred_element_type=jnp.float32
                )
                dk_acc[kv] += lax.dot_general(ds, query, tn, preferred_element_type=jnp.float32)

        @pl.when(jnp.logical_not(live))
        def _():
            ds_ref[side] = jnp.zeros(ds_ref.shape[1:], ds_ref.dtype)

    dk_ref[...] = (dk_acc[...] * scale).astype(dk_ref.dtype)
    dv_ref[...] = dv_acc[...].astype(dv_ref.dtype)


def chunk(scale, info, end, own, other, key, val, kind, name):
    rows, heads, size = own[0].shape
    width, kv_count = key.shape[:2]
    group = heads // kv_count
    acc = (kv_count, width, size)
    return pl.pallas_call(
        functools.partial(chunk_kernel, scale),
        in_specs=[SMEM] + [VMEM] * 9,
        out_specs=[VMEM] * 3,
        out_shape=[
            jax.ShapeDtypeStruct((2, kv_count, rows * group, width), jnp.bfloat16),
            jax.ShapeDtypeStruct(acc, kind),
            jax.ShapeDtypeStruct(acc, kind),
        ],
        scratch_shapes=[pltpu.VMEM(acc, jnp.float32), pltpu.VMEM(acc, jnp.float32)],
        compiler_params=params(32),
        name=name,
    )(info, end, *own, *other, key, val)


def query_kernel(scale, side, add, ds0, ds1, ds2, k0, k1, k2, *rest):
    out_ref = rest[-1]
    rows, heads, size = out_ref.shape
    kv_count = k0.shape[1]
    group = heads // kv_count
    for kv in range(kv_count):
        ds = jnp.concatenate([ds0[side, kv], ds1[side, kv], ds2[side, kv]], axis=1)
        key = jnp.concatenate([k0[:, kv, :], k1[:, kv, :], k2[:, kv, :]], axis=0)
        total = jnp.dot(ds, key, preferred_element_type=jnp.float32) * scale
        total = total.reshape(rows, group, size)
        span = slice(kv * group, (kv + 1) * group)
        if add:
            total = total + rest[0][:, span, :].astype(jnp.float32)
        out_ref[:, span, :] = total.astype(out_ref.dtype)


def query_grads(scale, side, ds, key, more, shape, name):
    return pl.pallas_call(
        functools.partial(query_kernel, scale, side, bool(more)),
        in_specs=[VMEM] * (6 + len(more)),
        out_specs=VMEM,
        out_shape=jax.ShapeDtypeStruct(shape, jnp.bfloat16),
        compiler_params=params(32),
        name=name,
    )(*ds, *key, *more)


def on_device(queries, keys, values, attn_out, out_grad, log_sums, doc_ids):
    width, heads, head_size = queries.shape
    scale = head_size ** (-0.5)
    count = lax.axis_size("seq")
    shard = lax.axis_index("seq")
    other = shard ^ 1

    def flip(value):
        return lax.ppermute(value, "seq", [(i, i ^ 1) for i in range(count)])

    def move(value, steps):
        return lax.ppermute(
            value, "seq", [(i, i + steps) for i in range(count) if 0 <= i + steps < count]
        )

    query_other, grad_other = flip(queries), flip(out_grad)
    key1, val1 = move(keys, 2), move(values, 2)
    key2, val2 = move(keys, 4), move(values, 4)
    logs4 = jnp.tile(log_sums.T * (head_size**0.5), (1, 128 // heads))
    aux = stats(out_grad, attn_out, logs4)
    aux_other = flip(aux)

    def bounds(distance):
        start = (shard - distance) * width
        docs = lax.dynamic_slice_in_dim(doc_ids, jnp.maximum(start, 0), width, 0)
        end = jnp.sum(doc_ids[None, :] <= docs[:, None], axis=1, dtype=jnp.int32) - 1
        end = jnp.where(start < 0, -1, end)
        info = jnp.stack([start, shard * width, other * width, end[-1]])
        return info, end[None, :]

    own = (queries, out_grad, aux)
    far = (query_other, grad_other, aux_other)
    ds0, dk0, dv0 = chunk(scale, *bounds(0), own, far, keys, values, jnp.float32, "chunk0")
    ds1, dk1, dv1 = chunk(scale, *bounds(2), own, far, key1, val1, jnp.bfloat16, "chunk1")
    dv1, dk1 = move(dv1, -2), move(dk1, -2)
    ds2, dk2, dv2 = chunk(scale, *bounds(4), own, far, key2, val2, jnp.bfloat16, "chunk2")
    dv2, dk2 = move(dv2, -4), move(dk2, -4)
    ds, ks = (ds0, ds1, ds2), (keys, key1, key2)
    part = query_grads(scale, 1, ds, ks, (), queries.shape, "query_other")
    query_grad = query_grads(scale, 0, ds, ks, (flip(part),), queries.shape, "query_own")

    def total(first, *rest):
        for one in rest:
            first = first + one.astype(jnp.float32)
        return first.astype(jnp.bfloat16).transpose(1, 0, 2)

    return query_grad, total(dk0, dk1, dk2), total(dv0, dv1, dv2)


def solution(mesh):
    rows = P(("dp", "seq"), None, None)
    return jax.shard_map(
        on_device,
        mesh=mesh,
        in_specs=(rows,) * 5 + (P(None, ("dp", "seq")), P("dp")),
        out_specs=(rows,) * 3,
        check_vma=False,
    )
```

```python
import functools

import jax
import jax.numpy as jnp
from jax import lax
from jax.experimental import pallas as pl
from jax.experimental.pallas import tpu as pltpu
from jax.sharding import PartitionSpec as P

COSTS = {
    "pack": 10,
    "prep": 10,
    "mid": 10,
    "far0": 10,
    "far1": 10,
    "near": 10,
    "query_other": 1,
    "query_own": 10,
    "sums": 10,
}
LOG2E = 1.4426950408889634
HBM = pl.BlockSpec(memory_space=pltpu.HBM)
VMEM = pl.BlockSpec(memory_space=pltpu.VMEM)
NT = (((1,), (1,)), ((), ()))
TN = (((0,), (0,)), ((), ()))
BF = jnp.bfloat16
F32 = jnp.float32


def call(kernel, name, shapes, operands, specs=None, scratch=(), after=(), mib=8):
    count = len(operands)

    def run(*refs):
        kernel(*refs[:count], *refs[count + len(after) :])

    return pl.pallas_call(
        run,
        in_specs=(specs or [VMEM] * count) + [VMEM] * len(after),
        out_specs=[VMEM] * len(shapes),
        out_shape=[jax.ShapeDtypeStruct(*one) for one in shapes],
        scratch_shapes=scratch,
        compiler_params=pltpu.CompilerParams(vmem_limit_bytes=mib * 1024 * 1024),
        cost_estimate=pl.CostEstimate(flops=int(COSTS[name] * 1e9), bytes_accessed=10**7, transcendentals=0),
        name=name,
    )(*operands, *after)


def split3(value):
    high = value.astype(BF).astype(F32)
    rest = value - high
    middle = rest.astype(BF).astype(F32)
    return high, middle, rest - middle


def start_copies(pairs, sems):
    copies = []
    for i, (source, target) in enumerate(pairs):
        copies.append(pltpu.make_async_copy(source, target, sems.at[i]))
        copies[-1].start()
    return copies


def pack_kernel(k_hbm, v_hbm, all_ref, k_ref, v_ref, sems):
    copies = start_copies(((k_hbm, k_ref), (v_hbm, v_ref)), sems)
    kv_count = k_ref.shape[1]
    for i, ref in enumerate((k_ref, v_ref)):
        copies[i].wait()
        for kv in range(kv_count):
            all_ref[i * kv_count + kv] = ref[:, kv, :]


def prep_kernel(halves, q_hbm, g_hbm, o_hbm, log_hbm, q1_ref, g1_ref, o1_ref, log1_ref, kv_ref, *refs):
    half_refs, (rows_ref, sub_ref, q_ref, g_ref, o_ref, log_ref, log_sem, sems) = refs[:halves], refs[halves:]
    rows, heads, size = q_ref.shape
    kv_count = rows_ref.shape[2]
    group = heads // kv_count
    each = kv_count // halves
    step = 32
    log_copy = start_copies(((log_hbm, log_ref),), log_sem)[0]
    copies = []
    for i, at in enumerate(range(0, rows, step)):
        part = pl.ds(at, step)
        pairs = [(one.at[part], two.at[part]) for one, two in ((g_hbm, g_ref), (o_hbm, o_ref), (q_hbm, q_ref))]
        copies.append(start_copies(pairs, sems.at[i]))
    for i, ref in enumerate(half_refs):
        ref[:each] = kv_ref[i * each : (i + 1) * each]
        ref[each:] = kv_ref[kv_count + i * each : kv_count + (i + 1) * each]
    lane_row = lax.broadcasted_iota(jnp.int32, (rows, 128), 1)
    lane = lax.broadcasted_iota(jnp.int32, (1, heads, 128), 2)
    head = lax.broadcasted_iota(jnp.int32, (1, heads, 128), 1)
    own = (lane == head) | (lane == head + heads) | (lane == head + 2 * heads)
    ones = jnp.where(lax.broadcasted_iota(jnp.int32, (128, 128), 0) < 3 * heads, 1.0, 0.0).astype(BF)
    for side, (q_one, g_one, o_one, log_one) in (
        (1, (q1_ref, g1_ref, o1_ref, log1_ref)),
        (0, (q_ref, g_ref, o_ref, log_ref)),
    ):
        if side == 0:
            log_copy.wait()
        logs = jnp.concatenate([log_one[...] * LOG2E] * (128 // heads), axis=0).T
        l_high, l_mid, l_low = split3(logs)
        logs = jnp.where(lane_row < heads, l_high, jnp.where(lane_row < 2 * heads, l_mid, l_low))
        for i, at in enumerate(range(0, rows, step)):
            part = slice(at, at + step)
            if side == 0:
                for one in copies[i]:
                    one.wait()
            grad, query = g_one[part], q_one[part]
            delta = jnp.sum(grad.astype(F32) * o_one[part].astype(F32), axis=-1, keepdims=True)
            delta = jnp.broadcast_to(delta, (step, heads, 128))
            aux = jnp.where(own, logs[part, None, :], 0.0).astype(BF)
            spot = slice(at * group, (at + step) * group)
            for kv in range(kv_count):
                span = slice(kv * group, (kv + 1) * group)
                rows_ref[side, 0, kv, spot] = query[:, span, :].reshape(step * group, size)
                rows_ref[side, 1, kv, spot] = grad[:, span, :].reshape(step * group, size)
                sub_ref[side, 0, kv, spot] = jnp.dot(
                    aux[:, span, :].reshape(step * group, 128), ones, preferred_element_type=F32
                )
                sub_ref[side, 1, kv, spot] = delta[:, span, :].reshape(step * group, 128)


def chunk_kernel(distance, first, doc_ref, rows_ref, sub_ref, kv_ref, ds_ref, out_ref, acc):
    count, size = rows_ref.shape[3:]
    each, width = kv_ref.shape[0] // 2, kv_ref.shape[1]
    rows = width
    scale = size ** (-0.5)
    shard = lax.axis_index("seq")
    key_shard = shard - distance
    key_doc = doc_ref[pl.ds(jnp.maximum(key_shard, 0), 1), :]
    acc[...] = jnp.zeros_like(acc)
    for side in range(2):
        query_shard = shard ^ side
        query_rows = jnp.broadcast_to(doc_ref[pl.ds(query_shard, 1), :], (rows, rows)).T
        ends = jnp.sum((query_rows <= key_doc).astype(jnp.int32), axis=0, keepdims=True)
        live = (key_shard >= 0) & (key_shard <= query_shard) & (jnp.max(ends) > 0)

        @pl.when(live)
        def _():
            pos = lax.broadcasted_iota(jnp.int32, (rows, count // rows, width), 0).reshape(count, width)
            low = (key_shard - query_shard) * width + lax.broadcasted_iota(jnp.int32, (1, width), 1)
            mask = (pos >= low) & (pos < ends)
            for j in range(each):
                query, grad = rows_ref[side, 0, first + j], rows_ref[side, 1, first + j]
                logits = lax.dot_general(query, kv_ref[j], NT, preferred_element_type=F32)
                logits = logits * (scale * LOG2E) - sub_ref[side, 0, first + j]
                probs = jnp.where(mask, jnp.exp2(logits), 0.0)
                diff = lax.dot_general(grad, kv_ref[each + j], NT, preferred_element_type=F32)
                ds = (probs * (diff - sub_ref[side, 1, first + j])).astype(BF)
                ds_ref[side, j] = ds
                sums = lax.dot_general(
                    jnp.concatenate([ds, probs.astype(BF)], axis=1),
                    jnp.concatenate([query, grad], axis=1),
                    TN,
                    preferred_element_type=F32,
                )
                acc[j] += sums[:width, :size] * scale
                acc[each + j] += sums[width:, size:]

        @pl.when(jnp.logical_not(live))
        def _():
            ds_ref[side] = jnp.zeros(ds_ref.shape[1:], BF)

    out_ref[...] = acc[...].astype(out_ref.dtype)


def query_kernel(side, parts, *refs):
    out_ref = refs[-1]
    total = sum(parts)
    rows, heads, size = out_ref.shape
    ds_refs, kv_refs = refs[:total], refs[total : 2 * total]
    firsts = [sum(parts[:i]) for i in range(len(parts))]
    kv_count = parts[0] * kv_refs[0].shape[0] // 2
    group = heads // kv_count

    def pick(kv, chunk):
        each = kv_count // parts[chunk]
        return firsts[chunk] + kv // each, kv % each

    for kv in range(kv_count):
        spots = [pick(kv, chunk) for chunk in range(len(parts))]
        ds = jnp.concatenate([ds_refs[i][side, j] for i, j in spots], axis=1)
        key = jnp.concatenate([kv_refs[i][j] for i, j in spots], axis=0)
        got = jnp.dot(ds, key, preferred_element_type=F32) * size ** (-0.5)
        out_ref[:, kv * group : (kv + 1) * group, :] = got.reshape(rows, group, size).astype(out_ref.dtype)


def near_kernel(parts, doc_ref, lay_ref, sub_ref, near_ref, *refs):
    rest, (ds_ref, out_ref, query_ref, acc) = refs[:-4], refs[-4:]
    chunk_kernel(0, 0, doc_ref, lay_ref, sub_ref, near_ref, ds_ref, out_ref, acc)
    more = sum(parts) - 1
    query_kernel(1, parts, ds_ref, *rest[:more], near_ref, *rest[more:], query_ref)


def sum_kernel(one_ref, two_ref, sums_ref, query_ref, key_ref, val_ref):
    query_ref[...] = (one_ref[...] + two_ref[...].astype(F32)).astype(BF)
    kv_count = key_ref.shape[1]
    for i, ref in enumerate((key_ref, val_ref)):
        heads = [sums_ref[i * kv_count + kv] for kv in range(kv_count)]
        ref[...] = jnp.stack(heads, axis=1).astype(BF)


def on_device(queries, keys, values, attn_out, out_grad, log_sums, doc_ids):
    width, heads, size = queries.shape
    kv_count = keys.shape[1]
    halves = 2
    each = kv_count // halves
    count = lax.axis_size("seq")
    docs = doc_ids.reshape(-1, width)
    rows = width * heads // kv_count
    half = (2 * each, width, size)
    full = (2 * kv_count, width, size)

    def flip(value):
        return lax.ppermute(value, "seq", [(i, i ^ 1) for i in range(count)])

    def move(value, steps):
        return lax.ppermute(
            value, "seq", [(i, i + steps) for i in range(count) if 0 <= i + steps < count]
        )

    hbm = functools.partial(pltpu.with_memory_space_constraint, memory_space=pltpu.HBM)
    (near,) = call(
        pack_kernel,
        "pack",
        [(full, BF)],
        (hbm(keys), hbm(values)),
        specs=[HBM] * 2,
        scratch=[pltpu.VMEM(keys.shape, BF)] * 2 + [pltpu.SemaphoreType.DMA((2,))],
    )
    mid = move(near, 2)
    own = (queries, out_grad, attn_out, log_sums)
    *halves_near, lay, sub = call(
        functools.partial(prep_kernel, halves),
        "prep",
        [(half, BF)] * halves + [((2, 2, kv_count, rows, size), BF), ((2, 2, kv_count, rows, 128), F32)],
        (*(hbm(one) for one in own), *(flip(one) for one in own), near),
        specs=[HBM] * 4 + [VMEM] * 5,
        scratch=[pltpu.VMEM(queries.shape, BF)] * 3
        + [pltpu.VMEM(log_sums.shape, F32)]
        + [pltpu.SemaphoreType.DMA((1,)), pltpu.SemaphoreType.DMA((width // 32, 3))],
        mib=24,
    )
    far = [move(one, 4) for one in halves_near]

    def chunk(kv, distance, first, kind, name, after=()):
        return call(
            functools.partial(chunk_kernel, distance, first),
            name,
            [((2, kv.shape[0] // 2, rows, width), BF), (kv.shape, kind)],
            (docs, lay, sub, kv),
            scratch=[pltpu.VMEM(kv.shape, F32)],
            after=after,
        )

    ds_mid, sums = chunk(mid, 2, 0, BF, "mid")
    mid_back = move(sums, -2)
    ds_far, far_back = [None] * halves, [None] * halves
    token = (ds_mid,)
    for index in reversed(range(halves)):
        ds_far[index], sums = chunk(far[index], 4, index * each, BF, "far" + str(index), token)
        token = (ds_far[index],)
        far_back[index] = move(sums, -4)
    parts = (1, 1, halves)
    rest = (ds_mid, *ds_far, mid, *far)
    ds_near, near_sums, part = call(
        functools.partial(near_kernel, parts),
        "near",
        [((2, kv_count, rows, width), BF), (full, F32), (queries.shape, BF)],
        (docs, lay, sub, near, *rest),
        scratch=[pltpu.VMEM(full, F32)],
    )
    rest = (ds_near, *rest[: 1 + halves], near, *rest[1 + halves :])
    (mine,) = call(functools.partial(query_kernel, 0, parts), "query_own", [(queries.shape, F32)], rest)
    far_sums = [one[:each] for one in far_back] + [one[each:] for one in far_back]
    sums = near_sums + mid_back.astype(F32) + jnp.concatenate(far_sums, axis=0).astype(F32)
    query_grad, key_grad, val_grad = call(
        sum_kernel,
        "sums",
        [(queries.shape, BF)] + [(keys.shape, BF)] * 2,
        (mine, flip(part), sums),
    )
    return query_grad, key_grad, val_grad


def solution(mesh):
    rows = P(("dp", "seq"), None, None)
    return jax.shard_map(
        on_device,
        mesh=mesh,
        in_specs=(rows,) * 5 + (P(None, ("dp", "seq")), P("dp")),
        out_specs=(rows,) * 3,
        check_vma=False,
    )
```

```python
import functools

import jax
import jax.numpy as jnp
from jax import lax
from jax.experimental import pallas as pl
from jax.experimental.pallas import tpu as pltpu
from jax.sharding import PartitionSpec as P

COSTS = {
    "pack": 10,
    "prep_early": 10,
    "prep_late": 10,
    "near_early": 10,
    "mid": 10,
    "far": 10,
    "near": 10,
    "query_own": 10,
    "sums": 10,
}
EARLY_HEADS = 4
LOG2E = 1.4426950408889634
HBM = pl.BlockSpec(memory_space=pltpu.HBM)
VMEM = pl.BlockSpec(memory_space=pltpu.VMEM)
NT = (((1,), (1,)), ((), ()))
TN = (((0,), (0,)), ((), ()))
BF = jnp.bfloat16
F32 = jnp.float32


def call(kernel, name, shapes, operands, specs=None, scratch=(), after=(), mib=8, aliases=None):
    count = len(operands)

    def run(*refs):
        kernel(*refs[:count], *refs[count + len(after) :])

    return pl.pallas_call(
        run,
        in_specs=(specs or [VMEM] * count) + [VMEM] * len(after),
        out_specs=[VMEM] * len(shapes),
        out_shape=[jax.ShapeDtypeStruct(*one) for one in shapes],
        scratch_shapes=scratch,
        compiler_params=pltpu.CompilerParams(vmem_limit_bytes=mib * 1024 * 1024),
        cost_estimate=pl.CostEstimate(flops=int(COSTS[name] * 1e9), bytes_accessed=10**7, transcendentals=0),
        input_output_aliases=aliases or {},
        name=name,
    )(*operands, *after)


def split3(value):
    high = value.astype(BF).astype(F32)
    rest = value - high
    middle = rest.astype(BF).astype(F32)
    return high, middle, rest - middle


def start_copies(pairs, sems):
    copies = []
    for i, (source, target) in enumerate(pairs):
        copies.append(pltpu.make_async_copy(source, target, sems.at[i]))
        copies[-1].start()
    return copies


def pack_kernel(k_hbm, v_hbm, all_ref, k_ref, v_ref, sems):
    copies = start_copies(((k_hbm, k_ref), (v_hbm, v_ref)), sems)
    kv_count = k_ref.shape[1]
    for i, ref in enumerate((k_ref, v_ref)):
        copies[i].wait()
        for kv in range(kv_count):
            all_ref[i * kv_count + kv] = ref[:, kv, :]


def prep_kernel(q_hbm, g_hbm, o_hbm, log_hbm, q1_ref, g1_ref, o1_ref, log1_ref, *refs):
    rows_ref, sub_ref, q_ref, g_ref, o_ref, log_ref, log_sem, sems = refs
    rows, heads, size = q_ref.shape
    kv_count = rows_ref.shape[2]
    group = heads // kv_count
    step = 32
    log_copy = start_copies(((log_hbm, log_ref),), log_sem)[0]
    copies = []
    for i, at in enumerate(range(0, rows, step)):
        part = pl.ds(at, step)
        pairs = [(one.at[part], two.at[part]) for one, two in ((g_hbm, g_ref), (o_hbm, o_ref), (q_hbm, q_ref))]
        copies.append(start_copies(pairs, sems.at[i]))
    lane_row = lax.broadcasted_iota(jnp.int32, (rows, 128), 1)
    lane = lax.broadcasted_iota(jnp.int32, (1, heads, 128), 2)
    head = lax.broadcasted_iota(jnp.int32, (1, heads, 128), 1)
    own = (lane == head) | (lane == head + heads) | (lane == head + 2 * heads)
    ones = jnp.where(lax.broadcasted_iota(jnp.int32, (128, 128), 0) < 3 * heads, 1.0, 0.0).astype(BF)
    for side, (q_one, g_one, o_one, log_one) in (
        (1, (q1_ref, g1_ref, o1_ref, log1_ref)),
        (0, (q_ref, g_ref, o_ref, log_ref)),
    ):
        if side == 0:
            log_copy.wait()
        logs = jnp.concatenate([log_one[...] * LOG2E] * (128 // heads), axis=0).T
        l_high, l_mid, l_low = split3(logs)
        logs = jnp.where(lane_row < heads, l_high, jnp.where(lane_row < 2 * heads, l_mid, l_low))
        for i, at in enumerate(range(0, rows, step)):
            part = slice(at, at + step)
            if side == 0:
                for one in copies[i]:
                    one.wait()
            grad, query = g_one[part], q_one[part]
            delta = jnp.sum(grad.astype(F32) * o_one[part].astype(F32), axis=-1, keepdims=True)
            delta = jnp.broadcast_to(delta, (step, heads, 128))
            aux = jnp.where(own, logs[part, None, :], 0.0).astype(BF)
            spot = slice(at * group, (at + step) * group)
            for kv in range(kv_count):
                span = slice(kv * group, (kv + 1) * group)
                rows_ref[side, 0, kv, spot] = query[:, span, :].reshape(step * group, size)
                rows_ref[side, 1, kv, spot] = grad[:, span, :].reshape(step * group, size)
                sub_ref[side, 0, kv, spot] = jnp.dot(
                    aux[:, span, :].reshape(step * group, 128), ones, preferred_element_type=F32
                )
                sub_ref[side, 1, kv, spot] = delta[:, span, :].reshape(step * group, 128)


def sends_far():
    return lax.axis_index("seq") + 4 < lax.axis_size("seq")


def prep_early_kernel(*refs):
    @pl.when(sends_far())
    def _():
        prep_kernel(*refs)


def prep_late_kernel(*refs):
    @pl.when(jnp.logical_not(sends_far()))
    def _():
        prep_kernel(*refs[:8], *refs[10:])


def chunk_kernel(distance, doc_ref, rows_ref, sub_ref, kv_ref, ds_ref, out_ref, acc, early=None):
    count, size = rows_ref.shape[3:]
    each, width = kv_ref.shape[0] // 2, kv_ref.shape[1]
    rows = width
    scale = size ** (-0.5)
    shard = lax.axis_index("seq")
    key_shard = shard - distance
    key_doc = doc_ref[pl.ds(jnp.maximum(key_shard, 0), 1), :]
    if early is None:
        acc[...] = jnp.zeros_like(acc)
    for side in range(2):
        query_shard = shard ^ side
        query_rows = jnp.broadcast_to(doc_ref[pl.ds(query_shard, 1), :], (rows, rows)).T
        ends = jnp.sum((query_rows <= key_doc).astype(jnp.int32), axis=0, keepdims=True)
        live = (key_shard >= 0) & (key_shard <= query_shard) & (jnp.max(ends) > 0)

        def heads(these):
            pos = lax.broadcasted_iota(jnp.int32, (rows, count // rows, width), 0).reshape(count, width)
            low = (key_shard - query_shard) * width + lax.broadcasted_iota(jnp.int32, (1, width), 1)
            mask = (pos >= low) & (pos < ends)
            for j in these:
                query, grad = rows_ref[side, 0, j], rows_ref[side, 1, j]
                logits = lax.dot_general(query, kv_ref[j], NT, preferred_element_type=F32)
                logits = logits * (scale * LOG2E) - sub_ref[side, 0, j]
                probs = jnp.where(mask, jnp.exp2(logits), 0.0)
                diff = lax.dot_general(grad, kv_ref[each + j], NT, preferred_element_type=F32)
                ds = (probs * (diff - sub_ref[side, 1, j])).astype(BF)
                ds_ref[side, j] = ds
                sums = lax.dot_general(
                    jnp.concatenate([ds, probs.astype(BF)], axis=1),
                    jnp.concatenate([query, grad], axis=1),
                    TN,
                    preferred_element_type=F32,
                )
                acc[j] += sums[:width, :size] * scale
                acc[each + j] += sums[width:, size:]

        if early == "only":
            if side == 0:
                heads(range(EARLY_HEADS))
            continue
        if early == "rest" and side == 0:
            pl.when(jnp.logical_not(sends_far()))(functools.partial(heads, range(EARLY_HEADS)))
            heads(range(EARLY_HEADS, each))
            continue
        pl.when(live)(functools.partial(heads, range(each)))

        @pl.when(jnp.logical_not(live))
        def _():
            ds_ref[side] = jnp.zeros(ds_ref.shape[1:], BF)

    out_ref[...] = acc[...].astype(out_ref.dtype)


def query_kernel(side, ds0_ref, ds1_ref, ds2_ref, kv0_ref, kv1_ref, kv2_ref, out_ref):
    rows, heads, size = out_ref.shape
    kv_count = kv0_ref.shape[0] // 2
    group = heads // kv_count
    for kv in range(kv_count):
        ds = jnp.concatenate([one[side, kv] for one in (ds0_ref, ds1_ref, ds2_ref)], axis=1)
        key = jnp.concatenate([one[kv] for one in (kv0_ref, kv1_ref, kv2_ref)], axis=0)
        got = jnp.dot(ds, key, preferred_element_type=F32) * size ** (-0.5)
        out_ref[:, kv * group : (kv + 1) * group, :] = got.reshape(rows, group, size).astype(out_ref.dtype)


def near_early_kernel(doc_ref, rows_ref, sub_ref, kv_ref, copy_ref, ds_ref, acc):
    copy_ref[...] = kv_ref[...]

    @pl.when(sends_far())
    def _():
        acc[...] = jnp.zeros_like(acc)
        chunk_kernel(0, doc_ref, rows_ref, sub_ref, kv_ref, ds_ref, acc, acc, "only")


def near_kernel(
    doc_ref, rows_ref, sub_ref, kv_ref, _, sums_in, ds1_ref, ds2_ref, kv1_ref, kv2_ref, ds_ref, out_ref, query_ref, acc
):
    acc[...] = jnp.zeros_like(acc)

    @pl.when(sends_far())
    def _():
        acc[...] = sums_in[...]

    chunk_kernel(0, doc_ref, rows_ref, sub_ref, kv_ref, ds_ref, out_ref, acc, "rest")
    query_kernel(1, ds_ref, ds1_ref, ds2_ref, kv_ref, kv1_ref, kv2_ref, query_ref)


def sum_kernel(one_ref, two_ref, sums_ref, query_ref, key_ref, val_ref):
    query_ref[...] = (one_ref[...] + two_ref[...].astype(F32)).astype(BF)
    kv_count = key_ref.shape[1]
    for i, ref in enumerate((key_ref, val_ref)):
        heads = [sums_ref[i * kv_count + kv] for kv in range(kv_count)]
        ref[...] = jnp.stack(heads, axis=1).astype(BF)


def on_device(queries, keys, values, attn_out, out_grad, log_sums, doc_ids):
    width, heads, size = queries.shape
    kv_count = keys.shape[1]
    count = lax.axis_size("seq")
    docs = doc_ids.reshape(-1, width)
    rows = width * heads // kv_count
    full = (2 * kv_count, width, size)

    def flip(value):
        return lax.ppermute(value, "seq", [(i, i ^ 1) for i in range(count)])

    def move(value, steps, parity=None):
        pairs = [(i, i + steps) for i in range(count) if 0 <= i + steps < count]
        return lax.ppermute(value, "seq", [one for one in pairs if parity in (None, one[0] // 2 % 2)])

    hbm = functools.partial(pltpu.with_memory_space_constraint, memory_space=pltpu.HBM)
    (near,) = call(
        pack_kernel,
        "pack",
        [(full, BF)],
        (hbm(keys), hbm(values)),
        specs=[HBM] * 2,
        scratch=[pltpu.VMEM(keys.shape, BF)] * 2 + [pltpu.SemaphoreType.DMA((2,))],
    )
    mid = move(near, 2)
    own = (queries, out_grad, attn_out, log_sums)
    own = tuple(hbm(one) for one in own) + tuple(flip(one) for one in own)
    laid = [((2, 2, kv_count, rows, size), BF), ((2, 2, kv_count, rows, 128), F32)]
    prep = dict(
        specs=[HBM] * 4 + [VMEM] * 4,
        scratch=[pltpu.VMEM(queries.shape, BF)] * 3
        + [pltpu.VMEM(log_sums.shape, F32)]
        + [pltpu.SemaphoreType.DMA((1,)), pltpu.SemaphoreType.DMA((width // 32, 3))],
        mib=24,
    )
    lay, sub = call(prep_early_kernel, "prep_early", laid, own, **prep)
    copied, ds_near, near_sums = call(
        near_early_kernel,
        "near_early",
        [(full, BF), ((2, kv_count, rows, width), BF), (full, F32)],
        (docs, lay, sub, near),
    )
    far = move(copied, 4)
    prep["specs"] = [HBM] * 4 + [VMEM] * 6
    lay, sub = call(prep_late_kernel, "prep_late", laid, (*own, lay, sub), aliases={8: 0, 9: 1}, **prep)

    def chunk(kv, distance, name, after=()):
        return call(
            functools.partial(chunk_kernel, distance),
            name,
            [((2, kv_count, rows, width), BF), (full, BF)],
            (docs, lay, sub, kv),
            scratch=[pltpu.VMEM(full, F32)],
            after=after,
        )

    ds_mid, mid_sums = chunk(mid, 2, "mid")
    mid_back = move(mid_sums, -2)
    ds_far, far_sums = chunk(far, 4, "far", (ds_mid,))
    far_back = move(far_sums, -4)
    ds_near, near_sums, part = call(
        near_kernel,
        "near",
        [((2, kv_count, rows, width), BF), (full, F32), (queries.shape, BF)],
        (docs, lay, sub, near, ds_near, near_sums, ds_mid, ds_far, mid, far),
        scratch=[pltpu.VMEM(full, F32)],
        aliases={4: 0},
    )
    (mine,) = call(
        functools.partial(query_kernel, 0),
        "query_own",
        [(queries.shape, F32)],
        (ds_near, ds_mid, ds_far, near, mid, far),
    )
    sums = near_sums + mid_back.astype(F32) + far_back.astype(F32)
    query_grad, key_grad, val_grad = call(
        sum_kernel,
        "sums",
        [(queries.shape, BF)] + [(keys.shape, BF)] * 2,
        (mine, flip(part), sums),
    )
    return query_grad, key_grad, val_grad


def solution(mesh):
    rows = P(("dp", "seq"), None, None)
    return jax.shard_map(
        on_device,
        mesh=mesh,
        in_specs=(rows,) * 5 + (P(None, ("dp", "seq")), P("dp")),
        out_specs=(rows,) * 3,
        check_vma=False,
    )
```

```python
import functools

import jax
import jax.numpy as jnp
from jax import lax
from jax.experimental import pallas as pl
from jax.experimental.pallas import tpu as pltpu
from jax.sharding import PartitionSpec as P

COSTS = {
    "pack": 10,
    "prep_early": 10,
    "prep_late": 10,
    "near_early": 10,
    "mid_even": 10,
    "mid_odd": 10,
    "far": 10,
    "near": 10,
    "query_own": 10,
    "sums": 10,
}
EARLY_HEADS = 4
LOG2E = 1.4426950408889634
HBM = pl.BlockSpec(memory_space=pltpu.HBM)
VMEM = pl.BlockSpec(memory_space=pltpu.VMEM)
NT = (((1,), (1,)), ((), ()))
TN = (((0,), (0,)), ((), ()))
BF = jnp.bfloat16
F32 = jnp.float32


def call(kernel, name, shapes, operands, specs=None, scratch=(), after=(), mib=8, aliases=None):
    count = len(operands)

    def run(*refs):
        kernel(*refs[:count], *refs[count + len(after) :])

    return pl.pallas_call(
        run,
        in_specs=(specs or [VMEM] * count) + [VMEM] * len(after),
        out_specs=[VMEM] * len(shapes),
        out_shape=[jax.ShapeDtypeStruct(*one) for one in shapes],
        scratch_shapes=scratch,
        compiler_params=pltpu.CompilerParams(vmem_limit_bytes=mib * 1024 * 1024),
        cost_estimate=pl.CostEstimate(flops=int(COSTS[name] * 1e9), bytes_accessed=10**7, transcendentals=0),
        input_output_aliases=aliases or {},
        name=name,
    )(*operands, *after)


def split3(value):
    high = value.astype(BF).astype(F32)
    rest = value - high
    middle = rest.astype(BF).astype(F32)
    return high, middle, rest - middle


def start_copies(pairs, sems):
    copies = []
    for i, (source, target) in enumerate(pairs):
        copies.append(pltpu.make_async_copy(source, target, sems.at[i]))
        copies[-1].start()
    return copies


def pack_kernel(k_hbm, v_hbm, all_ref, k_ref, v_ref, sems):
    copies = start_copies(((k_hbm, k_ref), (v_hbm, v_ref)), sems)
    kv_count = k_ref.shape[1]
    for i, ref in enumerate((k_ref, v_ref)):
        copies[i].wait()
        for kv in range(kv_count):
            all_ref[i * kv_count + kv] = ref[:, kv, :]


def prep_kernel(q_hbm, g_hbm, o_hbm, log_hbm, q1_ref, g1_ref, o1_ref, log1_ref, *refs):
    rows_ref, sub_ref, q_ref, g_ref, o_ref, log_ref, log_sem, sems = refs
    rows, heads, size = q_ref.shape
    kv_count = rows_ref.shape[2]
    group = heads // kv_count
    step = 32
    log_copy = start_copies(((log_hbm, log_ref),), log_sem)[0]
    copies = []
    for i, at in enumerate(range(0, rows, step)):
        part = pl.ds(at, step)
        pairs = [(one.at[part], two.at[part]) for one, two in ((g_hbm, g_ref), (o_hbm, o_ref), (q_hbm, q_ref))]
        copies.append(start_copies(pairs, sems.at[i]))
    lane_row = lax.broadcasted_iota(jnp.int32, (rows, 128), 1)
    lane = lax.broadcasted_iota(jnp.int32, (1, heads, 128), 2)
    head = lax.broadcasted_iota(jnp.int32, (1, heads, 128), 1)
    own = (lane == head) | (lane == head + heads) | (lane == head + 2 * heads)
    ones = jnp.where(lax.broadcasted_iota(jnp.int32, (128, 128), 0) < 3 * heads, 1.0, 0.0).astype(BF)
    for side, (q_one, g_one, o_one, log_one) in (
        (1, (q1_ref, g1_ref, o1_ref, log1_ref)),
        (0, (q_ref, g_ref, o_ref, log_ref)),
    ):
        if side == 0:
            log_copy.wait()
        logs = jnp.concatenate([log_one[...] * LOG2E] * (128 // heads), axis=0).T
        l_high, l_mid, l_low = split3(logs)
        logs = jnp.where(lane_row < heads, l_high, jnp.where(lane_row < 2 * heads, l_mid, l_low))
        for i, at in enumerate(range(0, rows, step)):
            part = slice(at, at + step)
            if side == 0:
                for one in copies[i]:
                    one.wait()
            grad, query = g_one[part], q_one[part]
            delta = jnp.sum(grad.astype(F32) * o_one[part].astype(F32), axis=-1, keepdims=True)
            delta = jnp.broadcast_to(delta, (step, heads, 128))
            aux = jnp.where(own, logs[part, None, :], 0.0).astype(BF)
            spot = slice(at * group, (at + step) * group)
            for kv in range(kv_count):
                span = slice(kv * group, (kv + 1) * group)
                rows_ref[side, 0, kv, spot] = query[:, span, :].reshape(step * group, size)
                rows_ref[side, 1, kv, spot] = grad[:, span, :].reshape(step * group, size)
                sub_ref[side, 0, kv, spot] = jnp.dot(
                    aux[:, span, :].reshape(step * group, 128), ones, preferred_element_type=F32
                )
                sub_ref[side, 1, kv, spot] = delta[:, span, :].reshape(step * group, 128)


def sends_far():
    return lax.axis_index("seq") + 4 < lax.axis_size("seq")


def prep_early_kernel(*refs):
    @pl.when(sends_far())
    def _():
        prep_kernel(*refs)


def prep_late_kernel(*refs):
    @pl.when(jnp.logical_not(sends_far()))
    def _():
        prep_kernel(*refs[:8], *refs[10:])


def mid_kernel(parity, *refs):
    @pl.when((lax.axis_index("seq") // 2) % 2 == parity)
    def _():
        chunk_kernel(2, *refs[:4], *refs[-3:])


def chunk_kernel(distance, doc_ref, rows_ref, sub_ref, kv_ref, ds_ref, out_ref, acc, early=None):
    count, size = rows_ref.shape[3:]
    each, width = kv_ref.shape[0] // 2, kv_ref.shape[1]
    rows = width
    scale = size ** (-0.5)
    shard = lax.axis_index("seq")
    key_shard = shard - distance
    key_doc = doc_ref[pl.ds(jnp.maximum(key_shard, 0), 1), :]
    if early is None:
        acc[...] = jnp.zeros_like(acc)
    for side in range(2):
        query_shard = shard ^ side
        query_rows = jnp.broadcast_to(doc_ref[pl.ds(query_shard, 1), :], (rows, rows)).T
        ends = jnp.sum((query_rows <= key_doc).astype(jnp.int32), axis=0, keepdims=True)
        live = (key_shard >= 0) & (key_shard <= query_shard) & (jnp.max(ends) > 0)

        def heads(these):
            pos = lax.broadcasted_iota(jnp.int32, (rows, count // rows, width), 0).reshape(count, width)
            low = (key_shard - query_shard) * width + lax.broadcasted_iota(jnp.int32, (1, width), 1)
            mask = (pos >= low) & (pos < ends)
            for j in these:
                query, grad = rows_ref[side, 0, j], rows_ref[side, 1, j]
                logits = lax.dot_general(query, kv_ref[j], NT, preferred_element_type=F32)
                logits = logits * (scale * LOG2E) - sub_ref[side, 0, j]
                probs = jnp.where(mask, jnp.exp2(logits), 0.0)
                diff = lax.dot_general(grad, kv_ref[each + j], NT, preferred_element_type=F32)
                ds = (probs * (diff - sub_ref[side, 1, j])).astype(BF)
                ds_ref[side, j] = ds
                sums = lax.dot_general(
                    jnp.concatenate([ds, probs.astype(BF)], axis=1),
                    jnp.concatenate([query, grad], axis=1),
                    TN,
                    preferred_element_type=F32,
                )
                acc[j] += sums[:width, :size] * scale
                acc[each + j] += sums[width:, size:]

        if early == "only":
            if side == 0:
                heads(range(EARLY_HEADS))
            continue
        if early == "rest" and side == 0:
            pl.when(jnp.logical_not(sends_far()))(functools.partial(heads, range(EARLY_HEADS)))
            heads(range(EARLY_HEADS, each))
            continue
        pl.when(live)(functools.partial(heads, range(each)))

        @pl.when(jnp.logical_not(live))
        def _():
            ds_ref[side] = jnp.zeros(ds_ref.shape[1:], BF)

    out_ref[...] = acc[...].astype(out_ref.dtype)


def query_kernel(side, ds0_ref, ds1_ref, ds2_ref, kv0_ref, kv1_ref, kv2_ref, out_ref):
    rows, heads, size = out_ref.shape
    kv_count = kv0_ref.shape[0] // 2
    group = heads // kv_count
    for kv in range(kv_count):
        ds = jnp.concatenate([one[side, kv] for one in (ds0_ref, ds1_ref, ds2_ref)], axis=1)
        key = jnp.concatenate([one[kv] for one in (kv0_ref, kv1_ref, kv2_ref)], axis=0)
        got = jnp.dot(ds, key, preferred_element_type=F32) * size ** (-0.5)
        out_ref[:, kv * group : (kv + 1) * group, :] = got.reshape(rows, group, size).astype(out_ref.dtype)


def near_early_kernel(doc_ref, rows_ref, sub_ref, kv_ref, copy_ref, ds_ref, acc):
    copy_ref[...] = kv_ref[...]

    @pl.when(sends_far())
    def _():
        acc[...] = jnp.zeros_like(acc)
        chunk_kernel(0, doc_ref, rows_ref, sub_ref, kv_ref, ds_ref, acc, acc, "only")


def near_kernel(
    doc_ref, rows_ref, sub_ref, kv_ref, _, sums_in, ds1_ref, ds2_ref, kv1_ref, kv2_ref, ds_ref, out_ref, query_ref, acc
):
    acc[...] = jnp.zeros_like(acc)

    @pl.when(sends_far())
    def _():
        acc[...] = sums_in[...]

    chunk_kernel(0, doc_ref, rows_ref, sub_ref, kv_ref, ds_ref, out_ref, acc, "rest")
    query_kernel(1, ds_ref, ds1_ref, ds2_ref, kv_ref, kv1_ref, kv2_ref, query_ref)


def sum_kernel(one_ref, two_ref, sums_ref, query_ref, key_ref, val_ref):
    query_ref[...] = (one_ref[...] + two_ref[...].astype(F32)).astype(BF)
    kv_count = key_ref.shape[1]
    for i, ref in enumerate((key_ref, val_ref)):
        heads = [sums_ref[i * kv_count + kv] for kv in range(kv_count)]
        ref[...] = jnp.stack(heads, axis=1).astype(BF)


def on_device(queries, keys, values, attn_out, out_grad, log_sums, doc_ids):
    width, heads, size = queries.shape
    kv_count = keys.shape[1]
    count = lax.axis_size("seq")
    docs = doc_ids.reshape(-1, width)
    rows = width * heads // kv_count
    full = (2 * kv_count, width, size)

    def flip(value):
        return lax.ppermute(value, "seq", [(i, i ^ 1) for i in range(count)])

    def move(value, steps, parity=None):
        pairs = [(i, i + steps) for i in range(count) if 0 <= i + steps < count]
        return lax.ppermute(value, "seq", [one for one in pairs if parity in (None, one[0] // 2 % 2)])

    hbm = functools.partial(pltpu.with_memory_space_constraint, memory_space=pltpu.HBM)
    (near,) = call(
        pack_kernel,
        "pack",
        [(full, BF)],
        (hbm(keys), hbm(values)),
        specs=[HBM] * 2,
        scratch=[pltpu.VMEM(keys.shape, BF)] * 2 + [pltpu.SemaphoreType.DMA((2,))],
    )
    mid = move(near, 2)
    own = (queries, out_grad, attn_out, log_sums)
    own = tuple(hbm(one) for one in own) + tuple(flip(one) for one in own)
    laid = [((2, 2, kv_count, rows, size), BF), ((2, 2, kv_count, rows, 128), F32)]
    prep = dict(
        specs=[HBM] * 4 + [VMEM] * 4,
        scratch=[pltpu.VMEM(queries.shape, BF)] * 3
        + [pltpu.VMEM(log_sums.shape, F32)]
        + [pltpu.SemaphoreType.DMA((1,)), pltpu.SemaphoreType.DMA((width // 32, 3))],
        mib=24,
    )
    lay, sub = call(prep_early_kernel, "prep_early", laid, own, **prep)
    copied, ds_near, near_sums = call(
        near_early_kernel,
        "near_early",
        [(full, BF), ((2, kv_count, rows, width), BF), (full, F32)],
        (docs, lay, sub, near),
    )
    far = move(copied, 4)
    prep["specs"] = [HBM] * 4 + [VMEM] * 6
    lay, sub = call(prep_late_kernel, "prep_late", laid, (*own, lay, sub), aliases={8: 0, 9: 1}, **prep)

    def chunk(kv, distance, name, after=()):
        return call(
            functools.partial(chunk_kernel, distance),
            name,
            [((2, kv_count, rows, width), BF), (full, BF)],
            (docs, lay, sub, kv),
            scratch=[pltpu.VMEM(full, F32)],
            after=after,
        )

    mid_shapes = [((2, kv_count, rows, width), BF), (full, BF)]
    mid_scratch = [pltpu.VMEM(full, F32)]
    ds_mid, even_sums = call(
        functools.partial(mid_kernel, 0), "mid_even", mid_shapes, (docs, lay, sub, mid), scratch=mid_scratch
    )
    even_back = move(even_sums, -2, 0)
    ds_mid, odd_sums = call(
        functools.partial(mid_kernel, 1),
        "mid_odd",
        mid_shapes,
        (docs, lay, sub, mid, ds_mid),
        scratch=mid_scratch,
        aliases={4: 0},
    )
    odd_back = move(odd_sums, -2, 1)
    ds_far, far_sums = chunk(far, 4, "far", (ds_mid,))
    far_back = move(far_sums, -4)
    ds_near, near_sums, part = call(
        near_kernel,
        "near",
        [((2, kv_count, rows, width), BF), (full, F32), (queries.shape, BF)],
        (docs, lay, sub, near, ds_near, near_sums, ds_mid, ds_far, mid, far),
        scratch=[pltpu.VMEM(full, F32)],
        aliases={4: 0},
        after=(even_back,),
    )
    (mine,) = call(
        functools.partial(query_kernel, 0),
        "query_own",
        [(queries.shape, F32)],
        (ds_near, ds_mid, ds_far, near, mid, far),
    )
    sums = near_sums + even_back.astype(F32) + odd_back.astype(F32) + far_back.astype(F32)
    query_grad, key_grad, val_grad = call(
        sum_kernel,
        "sums",
        [(queries.shape, BF)] + [(keys.shape, BF)] * 2,
        (mine, flip(part), sums),
    )
    return query_grad, key_grad, val_grad


def solution(mesh):
    rows = P(("dp", "seq"), None, None)
    return jax.shard_map(
        on_device,
        mesh=mesh,
        in_specs=(rows,) * 5 + (P(None, ("dp", "seq")), P("dp")),
        out_specs=(rows,) * 3,
        check_vma=False,
    )
```

```python
import functools

import jax
import jax.numpy as jnp
from jax import lax
from jax.experimental import pallas as pl
from jax.experimental.pallas import tpu as pltpu
from jax.sharding import PartitionSpec as P

COSTS = {
    "pack": 10,
    "prep_early": 10,
    "prep_late": 10,
    "near_early": 10,
    "mid_even": 10,
    "mid_odd": 10,
    "far": 10,
    "near": 10,
    "query_own": 10,
    "sums": 10,
}
EARLY_HEADS = 4
LOG2E = 1.4426950408889634
HBM = pl.BlockSpec(memory_space=pltpu.HBM)
VMEM = pl.BlockSpec(memory_space=pltpu.VMEM)
NT = (((1,), (1,)), ((), ()))
TN = (((0,), (0,)), ((), ()))
BF = jnp.bfloat16
F32 = jnp.float32


def call(kernel, name, shapes, operands, specs=None, scratch=(), after=(), mib=8, aliases=None):
    count = len(operands)

    def run(*refs):
        kernel(*refs[:count], *refs[count + len(after) :])

    return pl.pallas_call(
        run,
        in_specs=(specs or [VMEM] * count) + [VMEM] * len(after),
        out_specs=[VMEM] * len(shapes),
        out_shape=[jax.ShapeDtypeStruct(*one) for one in shapes],
        scratch_shapes=scratch,
        compiler_params=pltpu.CompilerParams(vmem_limit_bytes=mib * 1024 * 1024),
        cost_estimate=pl.CostEstimate(flops=int(COSTS[name] * 1e9), bytes_accessed=10**7, transcendentals=0),
        input_output_aliases=aliases or {},
        name=name,
    )(*operands, *after)


def split3(value):
    high = value.astype(BF).astype(F32)
    rest = value - high
    middle = rest.astype(BF).astype(F32)
    return high, middle, rest - middle


def start_copies(pairs, sems):
    copies = []
    for i, (source, target) in enumerate(pairs):
        copies.append(pltpu.make_async_copy(source, target, sems.at[i]))
        copies[-1].start()
    return copies


def pack_kernel(k_hbm, v_hbm, all_ref, k_ref, v_ref, sems):
    copies = start_copies(((k_hbm, k_ref), (v_hbm, v_ref)), sems)
    kv_count = k_ref.shape[1]
    for i, ref in enumerate((k_ref, v_ref)):
        copies[i].wait()
        for kv in range(kv_count):
            all_ref[i * kv_count + kv] = ref[:, kv, :]


def prep_kernel(q_hbm, g_hbm, o_hbm, log_hbm, q1_ref, g1_ref, o1_ref, log1_ref, *refs):
    rows_ref, sub_ref, q_ref, g_ref, o_ref, log_ref, log_sem, sems = refs
    rows, heads, size = q_ref.shape
    kv_count = rows_ref.shape[2]
    group = heads // kv_count
    step = 32
    log_copy = start_copies(((log_hbm, log_ref),), log_sem)[0]
    copies = []
    for i, at in enumerate(range(0, rows, step)):
        part = pl.ds(at, step)
        pairs = [(one.at[part], two.at[part]) for one, two in ((g_hbm, g_ref), (o_hbm, o_ref), (q_hbm, q_ref))]
        copies.append(start_copies(pairs, sems.at[i]))
    lane_row = lax.broadcasted_iota(jnp.int32, (rows, 128), 1)
    lane = lax.broadcasted_iota(jnp.int32, (1, heads, 128), 2)
    head = lax.broadcasted_iota(jnp.int32, (1, heads, 128), 1)
    own = (lane == head) | (lane == head + heads) | (lane == head + 2 * heads)
    ones = jnp.where(lax.broadcasted_iota(jnp.int32, (128, 128), 0) < 3 * heads, 1.0, 0.0).astype(BF)
    for side, (q_one, g_one, o_one, log_one) in (
        (1, (q1_ref, g1_ref, o1_ref, log1_ref)),
        (0, (q_ref, g_ref, o_ref, log_ref)),
    ):
        if side == 0:
            log_copy.wait()
        logs = jnp.concatenate([log_one[...] * LOG2E] * (128 // heads), axis=0).T
        l_high, l_mid, l_low = split3(logs)
        logs = jnp.where(lane_row < heads, l_high, jnp.where(lane_row < 2 * heads, l_mid, l_low))
        for i, at in enumerate(range(0, rows, step)):
            part = slice(at, at + step)
            if side == 0:
                for one in copies[i]:
                    one.wait()
            grad, query = g_one[part], q_one[part]
            delta = jnp.sum(grad.astype(F32) * o_one[part].astype(F32), axis=-1, keepdims=True)
            delta = jnp.broadcast_to(delta, (step, heads, 128))
            aux = jnp.where(own, logs[part, None, :], 0.0).astype(BF)
            spot = slice(at * group, (at + step) * group)
            for kv in range(kv_count):
                span = slice(kv * group, (kv + 1) * group)
                rows_ref[side, 0, kv, spot] = query[:, span, :].reshape(step * group, size)
                rows_ref[side, 1, kv, spot] = grad[:, span, :].reshape(step * group, size)
                sub_ref[side, 0, kv, spot] = jnp.dot(
                    aux[:, span, :].reshape(step * group, 128), ones, preferred_element_type=F32
                )
                sub_ref[side, 1, kv, spot] = delta[:, span, :].reshape(step * group, 128)


def sends_far():
    return lax.axis_index("seq") + 4 < lax.axis_size("seq")


def prep_early_kernel(*refs):
    @pl.when(sends_far())
    def _():
        prep_kernel(*refs)


def prep_late_kernel(doc_ref, *refs):
    ends_ref = refs[12]
    for step in range(3):
        for side in range(2):
            at = 2 * step + side
            ends_ref[at : at + 1, :] = ends_of(doc_ref, 2 * step, side)

    @pl.when(jnp.logical_not(sends_far()))
    def _():
        prep_kernel(*refs[:8], *refs[10:12], *refs[13:])


def mid_kernel(parity, *refs):
    @pl.when((lax.axis_index("seq") // 2) % 2 == parity)
    def _():
        chunk_kernel(2, *refs[:4], *refs[-3:])


def ends_of(doc_ref, distance, side):
    rows = doc_ref.shape[1]
    shard = lax.axis_index("seq")
    key_shard, query_shard = shard - distance, shard ^ side
    key_doc = doc_ref[pl.ds(jnp.maximum(key_shard, 0), 1), :]
    query_rows = jnp.broadcast_to(doc_ref[pl.ds(query_shard, 1), :], (rows, rows)).T
    ends = jnp.sum((query_rows <= key_doc).astype(jnp.int32), axis=0, keepdims=True)
    return jnp.where((key_shard >= 0) & (key_shard <= query_shard), ends, 0)


def chunk_kernel(distance, ends_ref, rows_ref, sub_ref, kv_ref, ds_ref, out_ref, acc, early=None):
    count, size = rows_ref.shape[3:]
    each, width = kv_ref.shape[0] // 2, kv_ref.shape[1]
    rows = width
    scale = size ** (-0.5)
    shard = lax.axis_index("seq")
    key_shard = shard - distance
    if early is None:
        acc[...] = jnp.zeros_like(acc)
    for side in range(2):
        query_shard = shard ^ side
        if early == "only":
            ends = ends_of(ends_ref, distance, side)
        else:
            ends = ends_ref[distance + side : distance + side + 1, :]
        live = jnp.max(ends) > 0

        def heads(these):
            pos = lax.broadcasted_iota(jnp.int32, (rows, count // rows, width), 0).reshape(count, width)
            low = (key_shard - query_shard) * width + lax.broadcasted_iota(jnp.int32, (1, width), 1)
            mask = (pos >= low) & (pos < ends)
            for j in these:
                query, grad = rows_ref[side, 0, j], rows_ref[side, 1, j]
                logits = lax.dot_general(query, kv_ref[j], NT, preferred_element_type=F32)
                logits = logits * (scale * LOG2E) - sub_ref[side, 0, j]
                probs = jnp.where(mask, jnp.exp2(logits), 0.0)
                diff = lax.dot_general(grad, kv_ref[each + j], NT, preferred_element_type=F32)
                ds = (probs * (diff - sub_ref[side, 1, j])).astype(BF)
                ds_ref[side, j] = ds
                sums = lax.dot_general(
                    jnp.concatenate([ds, probs.astype(BF)], axis=1),
                    jnp.concatenate([query, grad], axis=1),
                    TN,
                    preferred_element_type=F32,
                )
                acc[j] += sums[:width, :size] * scale
                acc[each + j] += sums[width:, size:]

        if early == "only":
            if side == 0:
                heads(range(EARLY_HEADS))
            continue
        if early == "rest" and side == 0:
            pl.when(jnp.logical_not(sends_far()))(functools.partial(heads, range(EARLY_HEADS)))
            heads(range(EARLY_HEADS, each))
            continue
        pl.when(live)(functools.partial(heads, range(each)))

        @pl.when(jnp.logical_not(live))
        def _():
            ds_ref[side] = jnp.zeros(ds_ref.shape[1:], BF)

    out_ref[...] = acc[...].astype(out_ref.dtype)


def query_kernel(side, ds0_ref, ds1_ref, ds2_ref, kv0_ref, kv1_ref, kv2_ref, out_ref):
    rows, heads, size = out_ref.shape
    kv_count = kv0_ref.shape[0] // 2
    group = heads // kv_count
    for kv in range(kv_count):
        ds = jnp.concatenate([one[side, kv] for one in (ds0_ref, ds1_ref, ds2_ref)], axis=1)
        key = jnp.concatenate([one[kv] for one in (kv0_ref, kv1_ref, kv2_ref)], axis=0)
        got = jnp.dot(ds, key, preferred_element_type=F32) * size ** (-0.5)
        out_ref[:, kv * group : (kv + 1) * group, :] = got.reshape(rows, group, size).astype(out_ref.dtype)


def near_early_kernel(doc_ref, rows_ref, sub_ref, kv_ref, copy_ref, ds_ref, acc):
    copy_ref[...] = kv_ref[...]

    @pl.when(sends_far())
    def _():
        acc[...] = jnp.zeros_like(acc)
        chunk_kernel(0, doc_ref, rows_ref, sub_ref, kv_ref, ds_ref, acc, acc, "only")


def near_kernel(
    doc_ref, rows_ref, sub_ref, kv_ref, _, sums_in, ds1_ref, ds2_ref, kv1_ref, kv2_ref, ds_ref, out_ref, query_ref, acc
):
    acc[...] = jnp.zeros_like(acc)

    @pl.when(sends_far())
    def _():
        acc[...] = sums_in[...]

    chunk_kernel(0, doc_ref, rows_ref, sub_ref, kv_ref, ds_ref, out_ref, acc, "rest")
    query_kernel(1, ds_ref, ds1_ref, ds2_ref, kv_ref, kv1_ref, kv2_ref, query_ref)


def sum_kernel(one_ref, two_ref, sums_ref, query_ref, key_ref, val_ref):
    query_ref[...] = (one_ref[...] + two_ref[...].astype(F32)).astype(BF)
    kv_count = key_ref.shape[1]
    for i, ref in enumerate((key_ref, val_ref)):
        heads = [sums_ref[i * kv_count + kv] for kv in range(kv_count)]
        ref[...] = jnp.stack(heads, axis=1).astype(BF)


def on_device(queries, keys, values, attn_out, out_grad, log_sums, doc_ids):
    width, heads, size = queries.shape
    kv_count = keys.shape[1]
    count = lax.axis_size("seq")
    docs = doc_ids.reshape(-1, width)
    rows = width * heads // kv_count
    full = (2 * kv_count, width, size)

    def flip(value):
        return lax.ppermute(value, "seq", [(i, i ^ 1) for i in range(count)])

    def move(value, steps, parity=None):
        pairs = [(i, i + steps) for i in range(count) if 0 <= i + steps < count]
        return lax.ppermute(value, "seq", [one for one in pairs if parity in (None, one[0] // 2 % 2)])

    hbm = functools.partial(pltpu.with_memory_space_constraint, memory_space=pltpu.HBM)
    (near,) = call(
        pack_kernel,
        "pack",
        [(full, BF)],
        (hbm(keys), hbm(values)),
        specs=[HBM] * 2,
        scratch=[pltpu.VMEM(keys.shape, BF)] * 2 + [pltpu.SemaphoreType.DMA((2,))],
    )
    mid = move(near, 2)
    own = (queries, out_grad, attn_out, log_sums)
    own = tuple(hbm(one) for one in own) + tuple(flip(one) for one in own)
    laid = [((2, 2, kv_count, rows, size), BF), ((2, 2, kv_count, rows, 128), F32)]
    prep = dict(
        specs=[HBM] * 4 + [VMEM] * 4,
        scratch=[pltpu.VMEM(queries.shape, BF)] * 3
        + [pltpu.VMEM(log_sums.shape, F32)]
        + [pltpu.SemaphoreType.DMA((1,)), pltpu.SemaphoreType.DMA((width // 32, 3))],
        mib=24,
    )
    lay, sub = call(prep_early_kernel, "prep_early", laid, own, **prep)
    copied, ds_near, near_sums = call(
        near_early_kernel,
        "near_early",
        [(full, BF), ((2, kv_count, rows, width), BF), (full, F32)],
        (docs, lay, sub, near),
    )
    far = move(copied, 4)
    prep["specs"] = [VMEM] + [HBM] * 4 + [VMEM] * 6
    lay, sub, ends = call(
        prep_late_kernel,
        "prep_late",
        [*laid, ((8, width), jnp.int32)],
        (docs, *own, lay, sub),
        aliases={9: 0, 10: 1},
        **prep,
    )

    def chunk(kv, distance, name, after=()):
        return call(
            functools.partial(chunk_kernel, distance),
            name,
            [((2, kv_count, rows, width), BF), (full, BF)],
            (ends, lay, sub, kv),
            scratch=[pltpu.VMEM(full, F32)],
            after=after,
        )

    mid_shapes = [((2, kv_count, rows, width), BF), (full, BF)]
    mid_scratch = [pltpu.VMEM(full, F32)]
    ds_mid, even_sums = call(
        functools.partial(mid_kernel, 0), "mid_even", mid_shapes, (ends, lay, sub, mid), scratch=mid_scratch
    )
    even_back = move(even_sums, -2, 0)
    ds_mid, odd_sums = call(
        functools.partial(mid_kernel, 1),
        "mid_odd",
        mid_shapes,
        (ends, lay, sub, mid, ds_mid),
        scratch=mid_scratch,
        aliases={4: 0},
    )
    odd_back = move(odd_sums, -2, 1)
    ds_far, far_sums = chunk(far, 4, "far", (ds_mid,))
    far_back = move(far_sums, -4)
    ds_near, near_sums, part = call(
        near_kernel,
        "near",
        [((2, kv_count, rows, width), BF), (full, F32), (queries.shape, BF)],
        (ends, lay, sub, near, ds_near, near_sums, ds_mid, ds_far, mid, far),
        scratch=[pltpu.VMEM(full, F32)],
        aliases={4: 0},
        after=(even_back,),
    )
    (mine,) = call(
        functools.partial(query_kernel, 0),
        "query_own",
        [(queries.shape, F32)],
        (ds_near, ds_mid, ds_far, near, mid, far),
    )
    sums = near_sums + even_back.astype(F32) + odd_back.astype(F32) + far_back.astype(F32)
    query_grad, key_grad, val_grad = call(
        sum_kernel,
        "sums",
        [(queries.shape, BF)] + [(keys.shape, BF)] * 2,
        (mine, flip(part), sums),
    )
    return query_grad, key_grad, val_grad


def solution(mesh):
    rows = P(("dp", "seq"), None, None)
    return jax.shard_map(
        on_device,
        mesh=mesh,
        in_specs=(rows,) * 5 + (P(None, ("dp", "seq")), P("dp")),
        out_specs=(rows,) * 3,
        check_vma=False,
    )
```

```python
import functools

import jax
import jax.numpy as jnp
from jax import lax
from jax.experimental import pallas as pl
from jax.experimental.pallas import tpu as pltpu
from jax.sharding import PartitionSpec as P

COSTS = {
    "pack": 10,
    "prep_early": 10,
    "prep_late": 10,
    "near_early": 10,
    "mid_even": 10,
    "mid_odd": 10,
    "far": 10,
    "near": 10,
    "query_own": 10,
    "sums": 10,
}
EARLY_HEADS = 4
LOG2E = 1.4426950408889634
HBM = pl.BlockSpec(memory_space=pltpu.HBM)
VMEM = pl.BlockSpec(memory_space=pltpu.VMEM)
NT = (((1,), (1,)), ((), ()))
TN = (((0,), (0,)), ((), ()))
BF = jnp.bfloat16
F32 = jnp.float32


def call(kernel, name, shapes, operands, specs=None, scratch=(), after=(), mib=8, aliases=None):
    count = len(operands)

    def run(*refs):
        kernel(*refs[:count], *refs[count + len(after) :])

    return pl.pallas_call(
        run,
        in_specs=(specs or [VMEM] * count) + [VMEM] * len(after),
        out_specs=[VMEM] * len(shapes),
        out_shape=[jax.ShapeDtypeStruct(*one) for one in shapes],
        scratch_shapes=scratch,
        compiler_params=pltpu.CompilerParams(vmem_limit_bytes=mib * 1024 * 1024),
        cost_estimate=pl.CostEstimate(flops=int(COSTS[name] * 1e9), bytes_accessed=10**7, transcendentals=0),
        input_output_aliases=aliases or {},
        name=name,
    )(*operands, *after)


def split3(value):
    high = value.astype(BF).astype(F32)
    rest = value - high
    middle = rest.astype(BF).astype(F32)
    return high, middle, rest - middle


def start_copies(pairs, sems):
    copies = []
    for i, (source, target) in enumerate(pairs):
        copies.append(pltpu.make_async_copy(source, target, sems.at[i]))
        copies[-1].start()
    return copies


def pack_kernel(k_hbm, v_hbm, all_ref, k_ref, v_ref, sems):
    rows, kv_count = k_ref.shape[:2]
    parts = [pl.ds(at, rows // 2) for at in (0, rows // 2)]
    pairs = [(one.at[part], two.at[part]) for part in parts for one, two in ((k_hbm, k_ref), (v_hbm, v_ref))]
    copies = start_copies(pairs, sems)
    for n, copy in enumerate(copies):
        copy.wait()
        part, ref = parts[n // 2], (k_ref, v_ref)[n % 2]
        for kv in range(kv_count):
            all_ref[n % 2 * kv_count + kv, part] = ref[part, kv, :]


def prep_kernel(q_hbm, g_hbm, o_hbm, log_hbm, q1_ref, g1_ref, o1_ref, log1_ref, *refs):
    rows_ref, sub_ref, q_ref, g_ref, o_ref, log_ref, log_sem, sems = refs
    rows, heads, size = q_ref.shape
    kv_count = rows_ref.shape[2]
    group = heads // kv_count
    step = 32
    log_copy = start_copies(((log_hbm, log_ref),), log_sem)[0]
    copies = []
    for i, at in enumerate(range(0, rows, step)):
        part = pl.ds(at, step)
        pairs = [(one.at[part], two.at[part]) for one, two in ((g_hbm, g_ref), (o_hbm, o_ref), (q_hbm, q_ref))]
        copies.append(start_copies(pairs, sems.at[i]))
    lane_row = lax.broadcasted_iota(jnp.int32, (rows, 128), 1)
    lane = lax.broadcasted_iota(jnp.int32, (1, heads, 128), 2)
    head = lax.broadcasted_iota(jnp.int32, (1, heads, 128), 1)
    own = (lane == head) | (lane == head + heads) | (lane == head + 2 * heads)
    ones = jnp.where(lax.broadcasted_iota(jnp.int32, (128, 128), 0) < 3 * heads, 1.0, 0.0).astype(BF)
    for side, (q_one, g_one, o_one, log_one) in (
        (1, (q1_ref, g1_ref, o1_ref, log1_ref)),
        (0, (q_ref, g_ref, o_ref, log_ref)),
    ):
        if side == 0:
            log_copy.wait()
        logs = jnp.concatenate([log_one[...] * LOG2E] * (128 // heads), axis=0).T
        l_high, l_mid, l_low = split3(logs)
        logs = jnp.where(lane_row < heads, l_high, jnp.where(lane_row < 2 * heads, l_mid, l_low))
        for i, at in enumerate(range(0, rows, step)):
            part = slice(at, at + step)
            if side == 0:
                for one in copies[i]:
                    one.wait()
            grad, query = g_one[part], q_one[part]
            delta = jnp.sum(grad.astype(F32) * o_one[part].astype(F32), axis=-1, keepdims=True)
            delta = jnp.broadcast_to(delta, (step, heads, 128))
            aux = jnp.where(own, logs[part, None, :], 0.0).astype(BF)
            spot = slice(at * group, (at + step) * group)
            for kv in range(kv_count):
                span = slice(kv * group, (kv + 1) * group)
                rows_ref[side, 0, kv, spot] = query[:, span, :].reshape(step * group, size)
                rows_ref[side, 1, kv, spot] = grad[:, span, :].reshape(step * group, size)
                sub_ref[side, 0, kv, spot] = jnp.dot(
                    aux[:, span, :].reshape(step * group, 128), ones, preferred_element_type=F32
                )
                sub_ref[side, 1, kv, spot] = delta[:, span, :].reshape(step * group, 128)


def sends_far():
    return lax.axis_index("seq") + 4 < lax.axis_size("seq")


def prep_early_kernel(*refs):
    @pl.when(sends_far())
    def _():
        prep_kernel(*refs)


def prep_late_kernel(doc_ref, *refs):
    ends_ref = refs[12]
    for step in range(3):
        for side in range(2):
            at = 2 * step + side
            ends_ref[at : at + 1, :] = ends_of(doc_ref, 2 * step, side)

    @pl.when(jnp.logical_not(sends_far()))
    def _():
        prep_kernel(*refs[:8], *refs[10:12], *refs[13:])


def mid_kernel(parity, *refs):
    @pl.when((lax.axis_index("seq") // 2) % 2 == parity)
    def _():
        chunk_kernel(2, *refs[:4], *refs[-3:])


def ends_of(doc_ref, distance, side):
    rows = doc_ref.shape[1]
    shard = lax.axis_index("seq")
    key_shard, query_shard = shard - distance, shard ^ side
    key_doc = doc_ref[pl.ds(jnp.maximum(key_shard, 0), 1), :]
    query_rows = jnp.broadcast_to(doc_ref[pl.ds(query_shard, 1), :], (rows, rows)).T
    ends = jnp.sum((query_rows <= key_doc).astype(jnp.int32), axis=0, keepdims=True)
    return jnp.where((key_shard >= 0) & (key_shard <= query_shard), ends, 0)


def chunk_kernel(distance, ends_ref, rows_ref, sub_ref, kv_ref, ds_ref, out_ref, acc, early=None):
    count, size = rows_ref.shape[3:]
    each, width = kv_ref.shape[0] // 2, kv_ref.shape[1]
    rows = width
    scale = size ** (-0.5)
    shard = lax.axis_index("seq")
    key_shard = shard - distance
    if early is None:
        acc[...] = jnp.zeros_like(acc)
    for side in range(2):
        query_shard = shard ^ side
        if early == "only":
            ends = ends_of(ends_ref, distance, side)
        else:
            ends = ends_ref[distance + side : distance + side + 1, :]
        live = jnp.max(ends) > 0

        def heads(these):
            pos = lax.broadcasted_iota(jnp.int32, (rows, count // rows, width), 0).reshape(count, width)
            low = (key_shard - query_shard) * width + lax.broadcasted_iota(jnp.int32, (1, width), 1)
            mask = (pos >= low) & (pos < ends)
            for j in these:
                query, grad = rows_ref[side, 0, j], rows_ref[side, 1, j]
                logits = lax.dot_general(query, kv_ref[j], NT, preferred_element_type=F32)
                logits = logits * (scale * LOG2E) - sub_ref[side, 0, j]
                probs = jnp.where(mask, jnp.exp2(logits), 0.0)
                diff = lax.dot_general(grad, kv_ref[each + j], NT, preferred_element_type=F32)
                ds = (probs * (diff - sub_ref[side, 1, j])).astype(BF)
                ds_ref[side, j] = ds
                sums = lax.dot_general(
                    jnp.concatenate([ds, probs.astype(BF)], axis=1),
                    jnp.concatenate([query, grad], axis=1),
                    TN,
                    preferred_element_type=F32,
                )
                acc[j] += sums[:width, :size] * scale
                acc[each + j] += sums[width:, size:]

        if early == "only":
            if side == 0:
                heads(range(EARLY_HEADS))
            continue
        if early == "rest" and side == 0:
            pl.when(jnp.logical_not(sends_far()))(functools.partial(heads, range(EARLY_HEADS)))
            heads(range(EARLY_HEADS, each))
            continue
        pl.when(live)(functools.partial(heads, range(each)))

        @pl.when(jnp.logical_not(live))
        def _():
            ds_ref[side] = jnp.zeros(ds_ref.shape[1:], BF)

    out_ref[...] = acc[...].astype(out_ref.dtype)


def query_kernel(side, ds0_ref, ds1_ref, ds2_ref, kv0_ref, kv1_ref, kv2_ref, out_ref):
    rows, heads, size = out_ref.shape
    kv_count = kv0_ref.shape[0] // 2
    group = heads // kv_count
    for kv in range(kv_count):
        ds = jnp.concatenate([one[side, kv] for one in (ds0_ref, ds1_ref, ds2_ref)], axis=1)
        key = jnp.concatenate([one[kv] for one in (kv0_ref, kv1_ref, kv2_ref)], axis=0)
        got = jnp.dot(ds, key, preferred_element_type=F32) * size ** (-0.5)
        out_ref[:, kv * group : (kv + 1) * group, :] = got.reshape(rows, group, size).astype(out_ref.dtype)


def near_early_kernel(doc_ref, rows_ref, sub_ref, kv_ref, copy_ref, ds_ref, acc):
    copy_ref[...] = kv_ref[...]

    @pl.when(sends_far())
    def _():
        acc[...] = jnp.zeros_like(acc)
        chunk_kernel(0, doc_ref, rows_ref, sub_ref, kv_ref, ds_ref, acc, acc, "only")


def near_kernel(
    doc_ref, rows_ref, sub_ref, kv_ref, _, sums_in, ds1_ref, ds2_ref, kv1_ref, kv2_ref, ds_ref, out_ref, query_ref, acc
):
    acc[...] = jnp.zeros_like(acc)

    @pl.when(sends_far())
    def _():
        acc[...] = sums_in[...]

    chunk_kernel(0, doc_ref, rows_ref, sub_ref, kv_ref, ds_ref, out_ref, acc, "rest")
    query_kernel(1, ds_ref, ds1_ref, ds2_ref, kv_ref, kv1_ref, kv2_ref, query_ref)


def sum_kernel(one_ref, two_ref, sums_ref, query_ref, key_ref, val_ref):
    query_ref[...] = (one_ref[...] + two_ref[...].astype(F32)).astype(BF)
    kv_count = key_ref.shape[1]
    for i, ref in enumerate((key_ref, val_ref)):
        heads = [sums_ref[i * kv_count + kv] for kv in range(kv_count)]
        ref[...] = jnp.stack(heads, axis=1).astype(BF)


def on_device(queries, keys, values, attn_out, out_grad, log_sums, doc_ids):
    width, heads, size = queries.shape
    kv_count = keys.shape[1]
    count = lax.axis_size("seq")
    docs = doc_ids.reshape(-1, width)
    rows = width * heads // kv_count
    full = (2 * kv_count, width, size)

    def flip(value):
        return lax.ppermute(value, "seq", [(i, i ^ 1) for i in range(count)])

    def move(value, steps, parity=None):
        pairs = [(i, i + steps) for i in range(count) if 0 <= i + steps < count]
        return lax.ppermute(value, "seq", [one for one in pairs if parity in (None, one[0] // 2 % 2)])

    hbm = functools.partial(pltpu.with_memory_space_constraint, memory_space=pltpu.HBM)
    (near,) = call(
        pack_kernel,
        "pack",
        [(full, BF)],
        (hbm(keys), hbm(values)),
        specs=[HBM] * 2,
        scratch=[pltpu.VMEM(keys.shape, BF)] * 2 + [pltpu.SemaphoreType.DMA((4,))],
    )
    mid = move(near, 2)
    own = (queries, out_grad, attn_out, log_sums)
    own = tuple(hbm(one) for one in own) + tuple(flip(one) for one in own)
    laid = [((2, 2, kv_count, rows, size), BF), ((2, 2, kv_count, rows, 128), F32)]
    prep = dict(
        specs=[HBM] * 4 + [VMEM] * 4,
        scratch=[pltpu.VMEM(queries.shape, BF)] * 3
        + [pltpu.VMEM(log_sums.shape, F32)]
        + [pltpu.SemaphoreType.DMA((1,)), pltpu.SemaphoreType.DMA((width // 32, 3))],
        mib=24,
    )
    lay, sub = call(prep_early_kernel, "prep_early", laid, own, **prep)
    copied, ds_near, near_sums = call(
        near_early_kernel,
        "near_early",
        [(full, BF), ((2, kv_count, rows, width), BF), (full, F32)],
        (docs, lay, sub, near),
    )
    far = move(copied, 4)
    prep["specs"] = [VMEM] + [HBM] * 4 + [VMEM] * 6
    lay, sub, ends = call(
        prep_late_kernel,
        "prep_late",
        [*laid, ((8, width), jnp.int32)],
        (docs, *own, lay, sub),
        aliases={9: 0, 10: 1},
        **prep,
    )

    def chunk(kv, distance, name, after=()):
        return call(
            functools.partial(chunk_kernel, distance),
            name,
            [((2, kv_count, rows, width), BF), (full, BF)],
            (ends, lay, sub, kv),
            scratch=[pltpu.VMEM(full, F32)],
            after=after,
        )

    mid_shapes = [((2, kv_count, rows, width), BF), (full, BF)]
    mid_scratch = [pltpu.VMEM(full, F32)]
    ds_mid, even_sums = call(
        functools.partial(mid_kernel, 0), "mid_even", mid_shapes, (ends, lay, sub, mid), scratch=mid_scratch
    )
    even_back = move(even_sums, -2, 0)
    ds_mid, odd_sums = call(
        functools.partial(mid_kernel, 1),
        "mid_odd",
        mid_shapes,
        (ends, lay, sub, mid, ds_mid),
        scratch=mid_scratch,
        aliases={4: 0},
    )
    odd_back = move(odd_sums, -2, 1)
    ds_far, far_sums = chunk(far, 4, "far", (ds_mid,))
    far_back = move(far_sums, -4)
    ds_near, near_sums, part = call(
        near_kernel,
        "near",
        [((2, kv_count, rows, width), BF), (full, F32), (queries.shape, BF)],
        (ends, lay, sub, near, ds_near, near_sums, ds_mid, ds_far, mid, far),
        scratch=[pltpu.VMEM(full, F32)],
        aliases={4: 0},
        after=(even_back,),
    )
    (mine,) = call(
        functools.partial(query_kernel, 0),
        "query_own",
        [(queries.shape, F32)],
        (ds_near, ds_mid, ds_far, near, mid, far),
    )
    sums = near_sums + even_back.astype(F32) + odd_back.astype(F32) + far_back.astype(F32)
    query_grad, key_grad, val_grad = call(
        sum_kernel,
        "sums",
        [(queries.shape, BF)] + [(keys.shape, BF)] * 2,
        (mine, flip(part), sums),
    )
    return query_grad, key_grad, val_grad


def solution(mesh):
    rows = P(("dp", "seq"), None, None)
    return jax.shard_map(
        on_device,
        mesh=mesh,
        in_specs=(rows,) * 5 + (P(None, ("dp", "seq")), P("dp")),
        out_specs=(rows,) * 3,
        check_vma=False,
    )
```

```python
import functools

import jax
import jax.numpy as jnp
from jax import lax
from jax.experimental import pallas as pl
from jax.experimental.pallas import tpu as pltpu
from jax.sharding import PartitionSpec as P

COSTS = {
    "pack": 10,
    "prep_early": 10,
    "prep_late": 10,
    "near_early": 10,
    "mid_even": 10,
    "mid_odd": 10,
    "far": 10,
    "near": 10,
    "query_own": 10,
    "sums": 10,
}
EARLY_HEADS = 4
LOG2E = 1.4426950408889634
HBM = pl.BlockSpec(memory_space=pltpu.HBM)
VMEM = pl.BlockSpec(memory_space=pltpu.VMEM)
NT = (((1,), (1,)), ((), ()))
TN = (((0,), (0,)), ((), ()))
BF = jnp.bfloat16
F32 = jnp.float32


def call(kernel, name, shapes, operands, specs=None, scratch=(), after=(), mib=8, aliases=None):
    count = len(operands)

    def run(*refs):
        kernel(*refs[:count], *refs[count + len(after) :])

    return pl.pallas_call(
        run,
        in_specs=(specs or [VMEM] * count) + [VMEM] * len(after),
        out_specs=[VMEM] * len(shapes),
        out_shape=[jax.ShapeDtypeStruct(*one) for one in shapes],
        scratch_shapes=scratch,
        compiler_params=pltpu.CompilerParams(vmem_limit_bytes=mib * 1024 * 1024),
        cost_estimate=pl.CostEstimate(flops=int(COSTS[name] * 1e9), bytes_accessed=10**7, transcendentals=0),
        input_output_aliases=aliases or {},
        name=name,
    )(*operands, *after)


def split3(value):
    high = value.astype(BF).astype(F32)
    rest = value - high
    middle = rest.astype(BF).astype(F32)
    return high, middle, rest - middle


def start_copies(pairs, sems):
    copies = []
    for i, (source, target) in enumerate(pairs):
        copies.append(pltpu.make_async_copy(source, target, sems.at[i]))
        copies[-1].start()
    return copies


def pack_kernel(k_hbm, v_hbm, all_ref, k_ref, v_ref, sems):
    copies = start_copies(((k_hbm, k_ref), (v_hbm, v_ref)), sems)
    kv_count = k_ref.shape[1]
    for i, ref in enumerate((k_ref, v_ref)):
        copies[i].wait()
        for kv in range(kv_count):
            all_ref[i * kv_count + kv] = ref[:, kv, :]


def prep_kernel(q_hbm, g_hbm, o_hbm, log_hbm, q1_ref, g1_ref, o1_ref, log1_ref, *refs):
    rows_ref, sub_ref, q_ref, g_ref, o_ref, log_ref, log_sem, sems = refs
    rows, heads, size = q_ref.shape
    kv_count = rows_ref.shape[2]
    group = heads // kv_count
    step = 32
    log_copy = start_copies(((log_hbm, log_ref),), log_sem)[0]
    copies = []
    for i, at in enumerate(range(0, rows, step)):
        part = pl.ds(at, step)
        pairs = [(one.at[part], two.at[part]) for one, two in ((g_hbm, g_ref), (o_hbm, o_ref), (q_hbm, q_ref))]
        copies.append(start_copies(pairs, sems.at[i]))
    lane_row = lax.broadcasted_iota(jnp.int32, (rows, 128), 1)
    lane = lax.broadcasted_iota(jnp.int32, (1, heads, 128), 2)
    head = lax.broadcasted_iota(jnp.int32, (1, heads, 128), 1)
    own = (lane == head) | (lane == head + heads) | (lane == head + 2 * heads)
    ones = jnp.where(lax.broadcasted_iota(jnp.int32, (128, 128), 0) < 3 * heads, 1.0, 0.0).astype(BF)
    for side, (q_one, g_one, o_one, log_one) in (
        (1, (q1_ref, g1_ref, o1_ref, log1_ref)),
        (0, (q_ref, g_ref, o_ref, log_ref)),
    ):
        if side == 0:
            log_copy.wait()
        logs = jnp.concatenate([log_one[...] * LOG2E] * (128 // heads), axis=0).T
        l_high, l_mid, l_low = split3(logs)
        logs = jnp.where(lane_row < heads, l_high, jnp.where(lane_row < 2 * heads, l_mid, l_low))
        for i, at in enumerate(range(0, rows, step)):
            part = slice(at, at + step)
            if side == 0:
                for one in copies[i]:
                    one.wait()
            grad, query = g_one[part], q_one[part]
            delta = jnp.sum(grad.astype(F32) * o_one[part].astype(F32), axis=-1, keepdims=True)
            delta = jnp.broadcast_to(delta, (step, heads, 128))
            aux = jnp.where(own, logs[part, None, :], 0.0).astype(BF)
            spot = slice(at * group, (at + step) * group)
            for kv in range(kv_count):
                span = slice(kv * group, (kv + 1) * group)
                rows_ref[side, 0, kv, spot] = query[:, span, :].reshape(step * group, size)
                rows_ref[side, 1, kv, spot] = grad[:, span, :].reshape(step * group, size)
                sub_ref[side, 0, kv, spot] = jnp.dot(
                    aux[:, span, :].reshape(step * group, 128), ones, preferred_element_type=F32
                )
                sub_ref[side, 1, kv, spot] = delta[:, span, :].reshape(step * group, 128)


def sends_far():
    return lax.axis_index("seq") + 4 < lax.axis_size("seq")


def prep_early_kernel(*refs):
    @pl.when(sends_far())
    def _():
        prep_kernel(*refs)


def prep_late_kernel(doc_ref, *refs):
    ends_ref = refs[12]
    for step in range(3):
        for side in range(2):
            at = 2 * step + side
            ends_ref[at : at + 1, :] = ends_of(doc_ref, 2 * step, side)

    @pl.when(jnp.logical_not(sends_far()))
    def _():
        prep_kernel(*refs[:8], *refs[10:12], *refs[13:])


def mid_kernel(parity, *refs):
    @pl.when((lax.axis_index("seq") // 2) % 2 == parity)
    def _():
        chunk_kernel(2, *refs[:4], *refs[-3:])


def ends_of(doc_ref, distance, side):
    rows = doc_ref.shape[1]
    shard = lax.axis_index("seq")
    key_shard, query_shard = shard - distance, shard ^ side
    key_doc = doc_ref[pl.ds(jnp.maximum(key_shard, 0), 1), :]
    query_rows = jnp.broadcast_to(doc_ref[pl.ds(query_shard, 1), :], (rows, rows)).T
    ends = jnp.sum((query_rows <= key_doc).astype(jnp.int32), axis=0, keepdims=True)
    return jnp.where((key_shard >= 0) & (key_shard <= query_shard), ends, 0)


def chunk_kernel(distance, ends_ref, rows_ref, sub_ref, kv_ref, ds_ref, out_ref, acc, early=None):
    count, size = rows_ref.shape[3:]
    each, width = kv_ref.shape[0] // 2, kv_ref.shape[1]
    rows = width
    scale = size ** (-0.5)
    shard = lax.axis_index("seq")
    key_shard = shard - distance
    if early is None:
        acc[...] = jnp.zeros_like(acc)
    for side in range(2):
        query_shard = shard ^ side
        if early == "only":
            ends = ends_of(ends_ref, distance, side)
        else:
            ends = ends_ref[distance + side : distance + side + 1, :]
        live = jnp.max(ends) > 0

        def heads(these):
            pos = lax.broadcasted_iota(jnp.int32, (rows, count // rows, width), 0).reshape(count, width)
            low = (key_shard - query_shard) * width + lax.broadcasted_iota(jnp.int32, (1, width), 1)
            mask = (pos >= low) & (pos < ends)
            for j in these:
                query, grad = rows_ref[side, 0, j], rows_ref[side, 1, j]
                logits = lax.dot_general(query, kv_ref[j], NT, preferred_element_type=F32)
                logits = logits * (scale * LOG2E) - sub_ref[side, 0, j]
                probs = jnp.where(mask, jnp.exp2(logits), 0.0)
                diff = lax.dot_general(grad, kv_ref[each + j], NT, preferred_element_type=F32)
                ds = (probs * (diff - sub_ref[side, 1, j])).astype(BF)
                ds_ref[side, j] = ds
                sums = lax.dot_general(
                    jnp.concatenate([ds, probs.astype(BF)], axis=1),
                    jnp.concatenate([query, grad], axis=1),
                    TN,
                    preferred_element_type=F32,
                )
                acc[j] += sums[:width, :size] * scale
                acc[each + j] += sums[width:, size:]

        if early == "only":
            if side == 0:
                heads(range(EARLY_HEADS))
            continue
        if early == "rest" and side == 0:
            pl.when(jnp.logical_not(sends_far()))(functools.partial(heads, range(EARLY_HEADS)))
            heads(range(EARLY_HEADS, each))
            continue
        pl.when(live)(functools.partial(heads, range(each)))

        @pl.when(jnp.logical_not(live))
        def _():
            ds_ref[side] = jnp.zeros(ds_ref.shape[1:], BF)

    out_ref[...] = acc[...].astype(out_ref.dtype)


def query_kernel(side, ds0_ref, ds1_ref, ds2_ref, kv0_ref, kv1_ref, kv2_ref, out_ref):
    rows, heads, size = out_ref.shape
    kv_count = kv0_ref.shape[0] // 2
    group = heads // kv_count
    for kv in range(kv_count):
        ds = jnp.concatenate([one[side, kv] for one in (ds0_ref, ds1_ref, ds2_ref)], axis=1)
        key = jnp.concatenate([one[kv] for one in (kv0_ref, kv1_ref, kv2_ref)], axis=0)
        got = jnp.dot(ds, key, preferred_element_type=F32) * size ** (-0.5)
        out_ref[:, kv * group : (kv + 1) * group, :] = got.reshape(rows, group, size).astype(out_ref.dtype)


def near_early_kernel(doc_ref, rows_ref, sub_ref, kv_ref, copy_ref, ds_ref, acc):
    copy_ref[...] = kv_ref[...]

    @pl.when(sends_far())
    def _():
        acc[...] = jnp.zeros_like(acc)
        chunk_kernel(0, doc_ref, rows_ref, sub_ref, kv_ref, ds_ref, acc, acc, "only")


def near_kernel(
    doc_ref, rows_ref, sub_ref, kv_ref, _, sums_in, ds1_ref, ds2_ref, kv1_ref, kv2_ref, ds_ref, out_ref, query_ref, acc
):
    acc[...] = jnp.zeros_like(acc)

    @pl.when(sends_far())
    def _():
        acc[...] = sums_in[...]

    chunk_kernel(0, doc_ref, rows_ref, sub_ref, kv_ref, ds_ref, out_ref, acc, "rest")
    query_kernel(1, ds_ref, ds1_ref, ds2_ref, kv_ref, kv1_ref, kv2_ref, query_ref)


def sum_kernel(one_ref, two_ref, sums_ref, query_ref, key_ref, val_ref):
    query_ref[...] = (one_ref[...] + two_ref[...].astype(F32)).astype(BF)
    kv_count = key_ref.shape[1]
    for i, ref in enumerate((key_ref, val_ref)):
        heads = [sums_ref[i * kv_count + kv].astype(BF) for kv in range(kv_count)]
        ref[...] = jnp.stack(heads, axis=1)


def on_device(queries, keys, values, attn_out, out_grad, log_sums, doc_ids):
    width, heads, size = queries.shape
    kv_count = keys.shape[1]
    count = lax.axis_size("seq")
    docs = doc_ids.reshape(-1, width)
    rows = width * heads // kv_count
    full = (2 * kv_count, width, size)

    def flip(value):
        return lax.ppermute(value, "seq", [(i, i ^ 1) for i in range(count)])

    def move(value, steps, parity=None):
        pairs = [(i, i + steps) for i in range(count) if 0 <= i + steps < count]
        return lax.ppermute(value, "seq", [one for one in pairs if parity in (None, one[0] // 2 % 2)])

    hbm = functools.partial(pltpu.with_memory_space_constraint, memory_space=pltpu.HBM)
    (near,) = call(
        pack_kernel,
        "pack",
        [(full, BF)],
        (hbm(keys), hbm(values)),
        specs=[HBM] * 2,
        scratch=[pltpu.VMEM(keys.shape, BF)] * 2 + [pltpu.SemaphoreType.DMA((2,))],
    )
    mid = move(near, 2)
    own = (queries, out_grad, attn_out, log_sums)
    own = tuple(hbm(one) for one in own) + tuple(flip(one) for one in own)
    laid = [((2, 2, kv_count, rows, size), BF), ((2, 2, kv_count, rows, 128), F32)]
    prep = dict(
        specs=[HBM] * 4 + [VMEM] * 4,
        scratch=[pltpu.VMEM(queries.shape, BF)] * 3
        + [pltpu.VMEM(log_sums.shape, F32)]
        + [pltpu.SemaphoreType.DMA((1,)), pltpu.SemaphoreType.DMA((width // 32, 3))],
        mib=24,
    )
    lay, sub = call(prep_early_kernel, "prep_early", laid, own, **prep)
    copied, ds_near, near_sums = call(
        near_early_kernel,
        "near_early",
        [(full, BF), ((2, kv_count, rows, width), BF), (full, F32)],
        (docs, lay, sub, near),
    )
    far = move(copied, 4)
    prep["specs"] = [VMEM] + [HBM] * 4 + [VMEM] * 6
    lay, sub, ends = call(
        prep_late_kernel,
        "prep_late",
        [*laid, ((8, width), jnp.int32)],
        (docs, *own, lay, sub),
        aliases={9: 0, 10: 1},
        **prep,
    )

    def chunk(kv, distance, name, after=()):
        return call(
            functools.partial(chunk_kernel, distance),
            name,
            [((2, kv_count, rows, width), BF), (full, BF)],
            (ends, lay, sub, kv),
            scratch=[pltpu.VMEM(full, F32)],
            after=after,
        )

    mid_shapes = [((2, kv_count, rows, width), BF), (full, BF)]
    mid_scratch = [pltpu.VMEM(full, F32)]
    ds_mid, even_sums = call(
        functools.partial(mid_kernel, 0), "mid_even", mid_shapes, (ends, lay, sub, mid), scratch=mid_scratch
    )
    even_back = move(even_sums, -2, 0)
    ds_mid, odd_sums = call(
        functools.partial(mid_kernel, 1),
        "mid_odd",
        mid_shapes,
        (ends, lay, sub, mid, ds_mid),
        scratch=mid_scratch,
        aliases={4: 0},
    )
    odd_back = move(odd_sums, -2, 1)
    ds_far, far_sums = chunk(far, 4, "far", (ds_mid,))
    far_back = move(far_sums, -4)
    ds_near, near_sums, part = call(
        near_kernel,
        "near",
        [((2, kv_count, rows, width), BF), (full, F32), (queries.shape, BF)],
        (ends, lay, sub, near, ds_near, near_sums, ds_mid, ds_far, mid, far),
        scratch=[pltpu.VMEM(full, F32)],
        aliases={4: 0},
        after=(even_back,),
    )
    (mine,) = call(
        functools.partial(query_kernel, 0),
        "query_own",
        [(queries.shape, F32)],
        (ds_near, ds_mid, ds_far, near, mid, far),
    )
    sums = near_sums + even_back.astype(F32) + odd_back.astype(F32) + far_back.astype(F32)
    query_grad, key_grad, val_grad = call(
        sum_kernel,
        "sums",
        [(queries.shape, BF)] + [(keys.shape, BF)] * 2,
        (mine, flip(part), sums),
    )
    return query_grad, key_grad, val_grad


def solution(mesh):
    rows = P(("dp", "seq"), None, None)
    return jax.shard_map(
        on_device,
        mesh=mesh,
        in_specs=(rows,) * 5 + (P(None, ("dp", "seq")), P("dp")),
        out_specs=(rows,) * 3,
        check_vma=False,
    )
```
